128 devices in a mesh: replica: 8 (over y_lo, z), fsdp: 16 (over x, y_hi, core).
Axes of the slice: x: 4, y: 4 (y_hi: 2, y_lo: 2; y = y_hi * 2 + y_lo), z: 4, core: 2. Of those that a mesh axis runs over, the one named last changes fastest.
Arguments:
- hidden_states: bfloat16 [32768, 8192], P(('replica', 'fsdp')), may hold values from -24 to 24
- key_weight: bfloat16 [8192, 1024], P('fsdp'), may hold values from -0.13258252 to 0.13258252
- previous_peak: float32 [1], replicated, may hold values from 0.088388346 to 0.12705825
- key_cotangent: bfloat16 [32768, 1024], P(('replica', 'fsdp')), may hold values from -6 to 6
Outputs:
- projected_keys: bfloat16 [32768, 1024], P(('replica', 'fsdp'))
- input_gradient: bfloat16 [32768, 8192], P(('replica', 'fsdp'))
- weight_gradient: bfloat16 [8192, 1024], P('fsdp')
- peak_ratio: float32 [1], replicated
The draws below stay inside these ranges and needn't reach their ends.
All inputs are finite; a program needn't handle non-finite values.
Results may differ from the reference program's by a relative error of at most 0.025.
Values may be sent and summed in bfloat16 or wider, within the bound.
A program may use at most 128 MiB of HBM per device.

```python
import jax
import jax.numpy as jnp
from jax import lax

D = 8192
KV = 1024
TOK_DEV = 256
TOKENS = 32768
N_REPLICA = 8
N_FSDP = 16


def draw_key_weight(key, part):
    key = jax.random.fold_in(key, 7)
    rising = 1.0 + 2.0 * jnp.arange(D, dtype=jnp.float32)[:, None] / (D - 1)
    base = jax.random.truncated_normal(key, -4.0, 4.0, (D, KV), jnp.float32)
    return (base * rising * D ** (-0.5)).astype(jnp.bfloat16)


def with_spikes(array, key, source, target, blocks, factor):
    def block_of(axis_at):
        return (jnp.arange(array.shape[axis_at]) // (array.shape[axis_at] // blocks)).reshape((-1,) + (1,) * (array.ndim - 1 - axis_at))

    one_side = jax.random.permutation(key, blocks)[block_of(target)]
    second = (block_of(target) + blocks // 2) % blocks
    return jnp.where((block_of(source) == one_side) | (block_of(source) == second), factor * array, array)


def levels(key, shape, pieces, least, largest):
    def one(dim, parts):
        heights = jax.random.uniform(jax.random.fold_in(jax.random.fold_in(key, 6), dim), (parts,), jnp.float32, least / len(pieces), largest / len(pieces))
        return jnp.repeat(jnp.exp(heights), shape[dim] // parts).reshape((-1,) + (1,) * (len(shape) - dim - 1))

    gain = one(*pieces[0])
    for cut in pieces[1:]:
        gain = gain * one(*cut)
    return gain


def noise(stream_key, dims, spread, reach, shards=(), kind=jnp.bfloat16):
    gain = levels(stream_key, dims, shards, -0.22, 0.18) if shards else 1.0
    result = jax.random.normal(stream_key, dims, jnp.float32) * spread * gain
    return jnp.minimum(jnp.maximum(result, -reach), reach).astype(kind)


def noise_with(stream_key, dims, scale, reach, shards, heavy, held_as=jnp.bfloat16):
    drawn = scale * jax.random.normal(stream_key, dims, jnp.float32)
    if shards:
        drawn = drawn * levels(stream_key, dims, shards, -0.22, 0.18)
    return jnp.clip(with_spikes(drawn, jax.random.fold_in(stream_key, 3), *heavy), -reach, reach).astype(held_as)


def setup_inputs(seed: int = 0) -> dict:
    seeds = jax.random.split(jax.random.key(seed), 5)
    hidden_states = noise_with(seeds[0], (TOKENS, D), 1.0, 24.0, ((0, 128),), (0, 1, 128, 5.5))
    key_weight = draw_key_weight(jax.random.fold_in(seeds[4], 71), 0)
    previous_peak = jnp.clip(jax.random.uniform(seeds[2], (1,), jnp.float32, 0.088388346, 0.12705825), 0.088388346, 0.12705825)
    key_cotangent = noise(seeds[3], (TOKENS, KV), 1.0, 6.0, ((0, 128),))
    return dict(hidden_states=hidden_states, key_weight=key_weight, previous_peak=previous_peak, key_cotangent=key_cotangent)


def quantize(weight, limit):
    return jnp.clip(weight.astype(jnp.float32) * (448.0 / limit), -448.0, 448.0).astype(jnp.bfloat16)


def reference(hidden_states, key_weight, previous_peak, key_cotangent):
    limit = previous_peak[0]
    unscale = limit / 448.0
    codes = quantize(key_weight, limit)
    projected_keys = (jnp.dot(hidden_states, codes, preferred_element_type=jnp.float32) * unscale).astype(jnp.bfloat16)
    input_gradient = (jnp.dot(key_cotangent, codes.T, preferred_element_type=jnp.float32) * unscale).astype(jnp.bfloat16)
    blocks_x = hidden_states.reshape(N_REPLICA, N_FSDP, TOK_DEV, D)
    blocks_g = key_cotangent.reshape(N_REPLICA, N_FSDP, TOK_DEV, KV)

    def device_step(acc, pair):
        term = jnp.dot(pair[0].T, pair[1], preferred_element_type=jnp.float32).astype(jnp.bfloat16)
        term = lax.optimization_barrier(term)
        return acc + term.astype(jnp.float32), None

    def replica_step(total, pair):
        group, unused = lax.scan(device_step, jnp.zeros((D, KV), jnp.float32), pair)
        rounded = lax.optimization_barrier(group.astype(jnp.bfloat16))
        return total + rounded.astype(jnp.float32), None

    total, unused = lax.scan(replica_step, jnp.zeros((D, KV), jnp.float32), (blocks_x, blocks_g))
    weight_gradient = (total * (TOKENS ** -0.5)).astype(jnp.bfloat16)
    peak = jnp.max(jnp.abs(key_weight.astype(jnp.float32)))
    peak_ratio = (peak / limit).reshape(1)
    return projected_keys, input_gradient, weight_gradient, peak_ratio
```

```python
import functools

import jax
import jax.numpy as jnp
from jax import lax
from jax.experimental import pallas as pl
from jax.experimental.pallas import tpu as pltpu
from jax.sharding import PartitionSpec as P

MESH = pl.DeviceIdType.MESH
AXES = ("x", "y", "z")
GATHER = ((0, 384, ("y", "z", "x")), (384, 384, ("z", "x", "y")), (768, 256, ("x", "y", "z")))
REDUCE = ((0, 384, ("x", "z", "y")), (384, 256, ("y", "x", "z")), (640, 384, ("z", "y", "x")))
ROWS = 64
WIDTH = 1024
TOK = 256
SLOTS = 8
BLOCK = 512


def position():
    replica, fsdp = lax.axis_index("replica"), lax.axis_index("fsdp")
    y_lo, z = replica // 4, lax.rem(replica, 4)
    x, y_hi, core = fsdp // 4, lax.rem(fsdp // 2, 2), lax.rem(fsdp, 2)
    return {"x": x, "y": y_hi * 2 + y_lo, "z": z}, core


def device(at, core):
    y_hi, y_lo = at["y"] // 2, lax.rem(at["y"], 2)
    return (y_lo * 4 + at["z"], at["x"] * 4 + y_hi * 2 + core)


def moved(at, axis, by):
    return {**at, axis: lax.rem(at[axis] + by, 4)}


def whole():
    return pl.ds(0, 4)


def in_order(order):
    return AXES.index(order[1]) < AXES.index(order[2])


def spot(k, slot, a, b):
    return (slot, a, b) if in_order(REDUCE[k][2]) else (slot, b, a)


def kernel(
    hidden, weight, limit, cotangent,
    keys_out, grad_out, wgrad_out, ratio_out,
    w_in, codes, partial, hid, cot, keys_acc, keys_send, keys_recv, grad_stage, total,
    peak, peak_in,
    r1a, r1b, r1c, r2a, r2b, r2c, r3a, r3b, r3c,
    load_sem, swap_send, swap_recv, ag_send, ag_recv, rs_send, rs_recv, rep_send, rep_recv,
    peak_send, peak_recv, key_send, key_recv, grad_local, grad_send, grad_recv, out_sem,
):
    at, core = position()
    other = 1 - core
    partner = device(at, other)
    f32, bf16 = jnp.float32, jnp.bfloat16

    def remote(src, dst, send, recv, to):
        return pltpu.make_async_remote_copy(
            src_ref=src, dst_ref=dst, send_sem=send, recv_sem=recv, device_id=to, device_id_type=MESH
        )

    y_lo = lax.rem(at["y"], 2)
    piece_row = pl.multiple_of((y_lo * 4 + at["z"]) * ROWS, ROWS)
    load_w = pltpu.make_async_copy(weight.at[pl.ds(piece_row, ROWS)], w_in, load_sem.at[0])
    load_w.start()
    load_c = pltpu.make_async_copy(cotangent, cot.at[core], load_sem.at[1])
    load_c.start()

    def hid_cols(slot, which):
        return pl.ds(pl.multiple_of((slot * 2 + which) * BLOCK, BLOCK), BLOCK)

    load_h = []
    for s in range(SLOTS):
        load_h.append(
            pltpu.make_async_copy(hidden.at[:, hid_cols(s, core)], hid.at[s, core], load_sem.at[2 + s])
        )
        load_h[-1].start()

    barrier = pltpu.get_barrier_semaphore()
    pl.semaphore_signal(barrier, inc=1, device_id=partner, device_id_type=MESH)
    for axis in AXES:
        for j in (1, 2, 3):
            pl.semaphore_signal(barrier, inc=1, device_id=device(moved(at, axis, j), core), device_id_type=MESH)
    pl.semaphore_wait(barrier, 10)

    load_w.wait()
    lim = jnp.full((1, WIDTH), limit[0], f32)
    w = w_in[...].astype(f32)
    codes[at["x"], at["y"], at["z"]] = jnp.clip(w * (448.0 / lim), -448.0, 448.0).astype(bf16)

    def view(ref, where, cols):
        return ref.at[where["x"], where["y"], where["z"], slice(None), cols]

    def gather_direct(k, phase):
        start, size, order = GATHER[k]
        where = dict(at)
        for axis in order[:phase]:
            where[axis] = whole()
        src = view(codes, where, pl.ds(start, size))
        copies = []
        for j in (1, 2, 3):
            n = phase * 3 + j - 1
            copies.append(
                remote(src, src, ag_send.at[k, n], ag_recv.at[k, n], device(moved(at, order[phase], j), core))
            )
        return copies

    sent = []

    def start(copies):
        for copy in copies:
            copy.start()
            sent.append(copy)

    ag0 = [gather_direct(k, 0) for k in range(3)]
    for copies in ag0:
        start(copies)

    swaps = [remote(cotangent, cot.at[core], swap_send.at[0], swap_recv.at[0], partner)]
    for s in range(SLOTS):
        swaps.append(
            remote(hidden.at[:, hid_cols(s, other)], hid.at[s, core], swap_send.at[1 + s], swap_recv.at[1 + s], partner)
        )
    start(swaps)

    peak[0] = jnp.max(jnp.abs(w).reshape(ROWS // 8, 8, WIDTH // 128, 128).max(axis=0), axis=1)
    def peak_phase(p):
        targets = [partner] if p == 3 else [device(moved(at, AXES[p], j), core) for j in (1, 2, 3)]
        copies = [
            remote(peak.at[p], peak_in.at[p, j], peak_send.at[p, j], peak_recv.at[p, j], to)
            for j, to in enumerate(targets)
        ]
        start(copies)
        return copies

    def peak_join(p, copies):
        best = peak[p]
        for j, copy in enumerate(copies):
            copy.wait_recv()
            best = jnp.maximum(best, peak_in[p, j])
        peak[p + 1] = best

    peaks = peak_phase(0)

    for copies in ag0:
        for copy in copies:
            copy.wait_recv()
    ag1 = [gather_direct(k, 1) for k in range(3)]
    for copies in ag1:
        start(copies)
    peak_join(0, peaks)
    peaks = peak_phase(1)

    load_c.wait()
    swaps[0].wait_recv()

    @pl.loop(0, SLOTS)
    def _(s):
        pltpu.make_async_copy(hidden.at[:, hid_cols(0, core)], hid.at[s, core], load_sem.at[2 + s]).wait()
        remote(hidden.at[:, hid_cols(0, other)], hid.at[s, core], swap_send.at[1 + s], swap_recv.at[1 + s], partner).wait_recv()
        h = hid[s].reshape(2 * TOK, BLOCK)
        for n in range(0, WIDTH, 512):
            term = lax.dot_general(
                h, cot[:, :, pl.ds(n, 512)].reshape(2 * TOK, 512), (((0,), (0,)), ((), ())), preferred_element_type=f32
            )
            partial[s // 2, pl.ds(lax.rem(s, 2) * 2, 2), :, :, pl.ds(n, 512)] = term.astype(bf16).reshape(2, 4, ROWS, 512)

    first_in, second_in, third_in = (r1a, r1b, r1c), (r2a, r2b, r2c), (r3a, r3b, r3c)

    def chunk(k, by, half):
        first, size, order = REDUCE[k]
        where = {axis: whole() for axis in AXES}
        where[order[0]] = lax.rem(at[order[0]] + by, 4)
        if half is not None:
            where[order[1]] = pl.ds(2 * half, 2)
        return where, pl.ds(first, size)

    def ring(k, n, by, half, slot):
        first, size, order = REDUCE[k]
        where, cols = chunk(k, by, half)
        to = device(moved(at, order[0], 1 if n % 2 == 0 else 3), core)
        return remote(view(partial, where, cols), first_in[k].at[slot], rs_send.at[k, n], rs_recv.at[k, n], to)

    rs0 = []
    for k in range(3):
        rs0.append([ring(k, 0, 2, 0, 0), ring(k, 1, 2, 1, 1), ring(k, 2, 1, 1, 2), ring(k, 3, 3, 0, 3)])
    for n in range(4):
        start([rs0[k][n] for k in range(3)])

    def rows_loop(fn):
        @pl.loop(0, 8)
        def _(i):
            fn(i // 4, lax.rem(i, 4))

    def part(k, by, half, a, b):
        first, size, order = REDUCE[k]
        where = {order[0]: lax.rem(at[order[0]] + by, 4), order[1]: 2 * half + a, order[2]: b}
        return (where["x"], where["y"], where["z"], slice(None), pl.ds(first, size))

    def add_far(k, n, by, half):
        rs0[k][n].wait_recv()

        def one(a, b):
            at_piece = part(k, by, half, a, b)
            partial[at_piece] = (partial[at_piece].astype(f32) + first_in[k][spot(k, n, a, b)].astype(f32)).astype(bf16)

        rows_loop(one)

    def gather_ring(k, n, by, half):
        first, size, order = GATHER[k]
        where = {axis: whole() for axis in AXES}
        where[order[2]] = lax.rem(at[order[2]] + by, 4)
        where[order[0]] = pl.ds(2 * half, 2)
        src = view(codes, where, pl.ds(first, size))
        to = device(moved(at, order[2], 1 if n % 2 == 0 else 3), core)
        return remote(src, src, ag_send.at[k, 6 + n], ag_recv.at[k, 6 + n], to)

    for copies in ag1:
        for copy in copies:
            copy.wait_recv()
    ag2 = [
        [gather_ring(k, 0, 0, 0), gather_ring(k, 1, 0, 1), gather_ring(k, 2, 0, 1), gather_ring(k, 3, 0, 0),
         gather_ring(k, 4, 3, 0), gather_ring(k, 5, 1, 1)]
        for k in range(3)
    ]
    for n in range(4):
        start([ag2[k][n] for k in range(3)])

    peak_join(1, peaks)
    peaks = peak_phase(2)

    rs1 = []
    for k in range(3):
        rs1.append([ring(k, 4, 1, 0, 4), ring(k, 5, 3, 1, 5)])
        add_far(k, 0, 1, 0)
        start([rs1[k][0]])
        add_far(k, 1, 3, 1)
        start([rs1[k][1]])

    for k in range(3):
        ag2[k][0].wait_recv()
        start([ag2[k][4]])
        ag2[k][1].wait_recv()
        start([ag2[k][5]])

    peak_join(2, peaks)
    peaks = peak_phase(3)

    def reduce_direct(k, phase):
        first, size, order = REDUCE[k]
        landing = second_in if phase == 1 else third_in
        copies = []
        for j in (1, 2, 3):
            where = {order[0]: at[order[0]], order[1]: at[order[1]], order[2]: whole()}
            where[order[phase]] = lax.rem(at[order[phase]] + j, 4)
            n = 6 + (phase - 1) * 3 + j - 1
            copies.append(
                remote(view(partial, where, pl.ds(first, size)), landing[k].at[j - 1], rs_send.at[k, n],
                       rs_recv.at[k, n], device(moved(at, order[phase], j), core))
            )
        return copies

    rs2 = []
    for k in range(3):
        for copy in (rs0[k][2], rs0[k][3], rs1[k][0], rs1[k][1]):
            copy.wait_recv()
        for half in (0, 1):
            near, far = (3, 4) if half == 0 else (2, 5)

            def one(a, b, k=k, half=half, near=near, far=far):
                at_piece = part(k, 0, half, a, b)
                partial[at_piece] = (
                    partial[at_piece].astype(f32)
                    + first_in[k][spot(k, near, a, b)].astype(f32)
                    + first_in[k][spot(k, far, a, b)].astype(f32)
                ).astype(bf16)

            rows_loop(one)
        rs2.append(reduce_direct(k, 1))
        start(rs2[k])

    for k in range(3):
        for n in range(2, 6):
            ag2[k][n].wait_recv()

    unscale = limit[0] * (1.0 / 448.0)
    keys_acc[...] = jnp.zeros_like(keys_acc)

    def grad_cols(s):
        return pl.ds(pl.multiple_of((s * 2 + core) * BLOCK, BLOCK), BLOCK)

    def slots(lo, hi):
        @pl.loop(lo, hi)
        def _(s):
            w_s = codes[s // 2, pl.ds(lax.rem(s, 2) * 2, 2)].reshape(BLOCK, WIDTH)
            h = hid[s].reshape(2 * TOK, BLOCK)
            for n in range(0, WIDTH, 512):
                keys_acc[:, pl.ds(n, 512)] += jnp.dot(h, w_s[:, n : n + 512], preferred_element_type=f32)
            c_all = cot[...].reshape(2 * TOK, WIDTH)
            for n in range(0, BLOCK, 256):
                g = lax.dot_general(
                    c_all, w_s[n : n + 256], (((1,), (1,)), ((), ())), preferred_element_type=f32
                )
                grad_stage[s, :, :, pl.ds(n, 256)] = (g * unscale).astype(bf16).reshape(2, TOK, 256)
            pltpu.make_async_copy(grad_stage.at[s, core], grad_out.at[:, grad_cols(s)], grad_local.at[s]).start()
            remote(grad_stage.at[s, other], grad_out.at[:, grad_cols(s)], grad_send.at[s], grad_recv.at[s], partner).start()

    slots(0, 4)

    rs3 = []
    for k in range(3):
        first, size, order = REDUCE[k]
        for copy in rs2[k]:
            copy.wait_recv()

        @pl.loop(0, 4)
        def _(b, k=k, first=first, size=size, order=order):
            where = {order[0]: at[order[0]], order[1]: at[order[1]], order[2]: b}
            at_piece = (where["x"], where["y"], where["z"], slice(None), pl.ds(first, size))
            acc = partial[at_piece].astype(f32)
            for j in range(3):
                acc += second_in[k][j, b].astype(f32)
            partial[at_piece] = acc.astype(bf16)

        rs3.append(reduce_direct(k, 2))
        start(rs3[k])

    slots(4, 8)

    keys_send[...] = keys_acc[pl.ds(pl.multiple_of(other * TOK, TOK), TOK)].astype(bf16)
    key_copy = remote(keys_send, keys_recv, key_send.at[0], key_recv.at[0], partner)
    start([key_copy])

    for k in range(3):
        first, size, order = REDUCE[k]
        for copy in rs3[k]:
            copy.wait_recv()
        acc = partial[at["x"], at["y"], at["z"], :, pl.ds(first, size)].astype(f32)
        for j in range(3):
            acc += third_in[k][j].astype(f32)
        total[:, pl.ds(first, size)] = (acc * (32768.0**-0.5)).astype(bf16)

    def piece(lo, z):
        return wgrad_out.at[pl.ds(pl.multiple_of((lo * 4 + z) * ROWS, ROWS), ROWS)]

    beside = {**at, "y": at["y"] + 1 - 2 * y_lo}
    own = pltpu.make_async_copy(total, piece(y_lo, at["z"]), out_sem.at[0])
    own.start()
    rep0 = [
        remote(total, piece(y_lo, at["z"]), rep_send.at[0], rep_recv.at[0], device(beside, core)),
        remote(total, piece(y_lo, at["z"]), rep_send.at[1], rep_recv.at[1], device(moved(at, "z", 1), core)),
        remote(total, piece(y_lo, at["z"]), rep_send.at[2], rep_recv.at[2], device(moved(at, "z", 3), core)),
        remote(total, piece(y_lo, at["z"]), rep_send.at[3], rep_recv.at[3], device(moved(at, "z", 2), core)),
    ]
    start(rep0)

    peak_join(3, peaks)
    ratio_out[0] = jnp.max(peak[4] / jnp.full((8, 128), limit[0], f32))
    key_copy.wait_recv()
    mine = keys_acc[pl.ds(pl.multiple_of(core * TOK, TOK), TOK)] + keys_recv[...].astype(f32)
    keys_send_2 = (mine * unscale).astype(bf16)
    key_copy.wait_send()
    keys_send[...] = keys_send_2
    sent[:] = [copy for copy in sent if copy is not key_copy]
    out_keys = pltpu.make_async_copy(keys_send, keys_out, out_sem.at[1])
    out_keys.start()

    z_far = lax.rem(at["z"] + 2, 4)
    rep0[0].wait_recv()
    across = piece(1 - y_lo, at["z"])
    rep1 = [
        remote(across, across, rep_send.at[4], rep_recv.at[4], device(moved(at, "z", 1), core)),
        remote(across, across, rep_send.at[5], rep_recv.at[5], device(moved(at, "z", 3), core)),
    ]
    start(rep1)
    rep0[3].wait_recv()
    far = piece(y_lo, z_far)
    rep1.append(remote(far, far, rep_send.at[6], rep_recv.at[6], device(beside, core)))
    start(rep1[2:])
    for copy in (rep0[1], rep0[2], *rep1):
        copy.wait_recv()

    for s in range(SLOTS):
        pltpu.make_async_copy(grad_stage.at[s, core], grad_out.at[:, grad_cols(s)], grad_local.at[s]).wait()
        remote(grad_stage.at[s, other], grad_out.at[:, grad_cols(s)], grad_send.at[s], grad_recv.at[s], partner).wait()
    own.wait()
    out_keys.wait()
    for copy in sent:
        copy.wait_send()


def landing(k, phase):
    first, size, order = REDUCE[k]
    if phase == 0:
        return pltpu.VMEM((*spot(k, 6, 2, 4), ROWS, size), jnp.bfloat16)
    if phase == 1:
        return pltpu.VMEM((3, 4, ROWS, size), jnp.bfloat16)
    return pltpu.VMEM((3, ROWS, size), jnp.bfloat16)


def body(hidden_states, key_weight, previous_peak, key_cotangent):
    bf16, f32 = jnp.bfloat16, jnp.float32
    any_space = pl.BlockSpec(memory_space=pl.ANY)
    smem = pl.BlockSpec(memory_space=pltpu.SMEM)
    dma = pltpu.SemaphoreType.DMA
    return pl.pallas_call(
        kernel,
        out_shape=(
            jax.ShapeDtypeStruct((TOK, WIDTH), bf16),
            jax.ShapeDtypeStruct((TOK, 2 * SLOTS * BLOCK), bf16),
            jax.ShapeDtypeStruct((BLOCK, WIDTH), bf16),
            jax.ShapeDtypeStruct((1,), f32),
        ),
        in_specs=[any_space, any_space, smem, any_space],
        out_specs=(any_space, any_space, any_space, smem),
        scratch_shapes=[
            pltpu.VMEM((ROWS, WIDTH), bf16),
            pltpu.VMEM((4, 4, 4, ROWS, WIDTH), bf16),
            pltpu.VMEM((4, 4, 4, ROWS, WIDTH), bf16),
            pltpu.VMEM((SLOTS, 2, TOK, BLOCK), bf16),
            pltpu.VMEM((2, TOK, WIDTH), bf16),
            pltpu.VMEM((2 * TOK, WIDTH), f32),
            pltpu.VMEM((TOK, WIDTH), bf16),
            pltpu.VMEM((TOK, WIDTH), bf16),
            pltpu.VMEM((SLOTS, 2, TOK, BLOCK), bf16),
            pltpu.VMEM((ROWS, WIDTH), bf16),
            pltpu.VMEM((5, 8, 128), f32),
            pltpu.VMEM((4, 3, 8, 128), f32),
            *[landing(k, phase) for phase in range(3) for k in range(3)],
            dma((2 + SLOTS,)),
            dma((1 + SLOTS,)),
            dma((1 + SLOTS,)),
            dma((3, 12)),
            dma((3, 12)),
            dma((3, 12)),
            dma((3, 12)),
            dma((7,)),
            dma((7,)),
            dma((4, 3)),
            dma((4, 3)),
            dma((1,)),
            dma((1,)),
            dma((SLOTS,)),
            dma((SLOTS,)),
            dma((SLOTS,)),
            dma((2,)),
        ],
        compiler_params=pltpu.CompilerParams(
            collective_id=0, has_side_effects=True, vmem_limit_bytes=58 * 2**20
        ),
    )(hidden_states, key_weight, previous_peak, key_cotangent)


def solution(mesh):
    in_specs = (P(("replica", "fsdp"), None), P("fsdp", None), P(), P(("replica", "fsdp"), None))
    out_specs = (P(("replica", "fsdp"), None), P(("replica", "fsdp"), None), P("fsdp", None), P())
    return jax.shard_map(body, mesh=mesh, in_specs=in_specs, out_specs=out_specs, check_vma=False)
```

```python
import jax
import jax.numpy as jnp
from jax import lax
from jax.experimental import pallas as pl
from jax.experimental.pallas import tpu as pltpu
from jax.sharding import PartitionSpec as P

MESH = pl.DeviceIdType.MESH
AXES = ("x", "y", "z")
ROWS = 64
WIDTH = 1024
TOK = 256
SLOTS = 8
BLOCK = 512
GATHER = ((0, 256, ("z", "y", "x")), (256, 384, ("z", "x", "y")), (640, 384, ("y", "x", "z")))
REDUCE = (
    (0, 640, 384, ("z", "x", "y")),
    (0, 0, 384, ("x", "y", "z")),
    (0, 384, 256, ("y", "z", "x")),
    (1, 640, 384, ("z", "y", "x")),
    (1, 0, 256, ("x", "z", "y")),
    (1, 256, 384, ("y", "x", "z")),
)
GROUPS = len(REDUCE)
HALF = ROWS // 2


def position():
    replica, fsdp = lax.axis_index("replica"), lax.axis_index("fsdp")
    y_lo, z = replica // 4, lax.rem(replica, 4)
    x, y_hi, core = fsdp // 4, lax.rem(fsdp // 2, 2), lax.rem(fsdp, 2)
    return {"x": x, "y": y_hi * 2 + y_lo, "z": z}, core


def device(at, core):
    y_hi, y_lo = at["y"] // 2, lax.rem(at["y"], 2)
    return (y_lo * 4 + at["z"], at["x"] * 4 + y_hi * 2 + core)


def moved(at, axis, by):
    return {**at, axis: lax.rem(at[axis] + by, 4)}


def whole():
    return pl.ds(0, 4)


def spot(k, slot, a, b):
    order = REDUCE[k][3]
    return (slot, a, b) if AXES.index(order[1]) < AXES.index(order[2]) else (slot, b, a)


def half_rows(half):
    return pl.ds(half * HALF, HALF)


def kernel(hidden, weight, limit, cotangent, keys_out, grad_out, wgrad_out, ratio_out, *scratch):
    (w_in, codes, partial, hid, cot, keys_acc, keys_send, keys_recv, grad_stage, peak, peak_in) = scratch[:11]
    landings = scratch[11 : 11 + 3 * GROUPS]
    first_in, second_in, third_in = (landings[n * GROUPS : (n + 1) * GROUPS] for n in range(3))
    (load_sem, swap_send, swap_recv, ag_send, ag_recv, rs_send, rs_recv, rep_send, rep_recv,
     peak_send, peak_recv, key_send, key_recv, grad_send, grad_recv) = scratch[11 + 3 * GROUPS :]

    at, core = position()
    other = 1 - core
    partner = device(at, other)
    f32, bf16 = jnp.float32, jnp.bfloat16
    y_lo = lax.rem(at["y"], 2)

    def remote(src, dst, send, recv, to):
        return pltpu.make_async_remote_copy(
            src_ref=src, dst_ref=dst, send_sem=send, recv_sem=recv, device_id=to, device_id_type=MESH
        )

    sent = []

    def start(copies):
        for copy in copies:
            copy.start()
            sent.append(copy)

    def hid_cols(slot, which):
        return pl.ds(pl.multiple_of((slot * 2 + which) * BLOCK, BLOCK), BLOCK)

    load_w = pltpu.make_async_copy(
        weight.at[pl.ds(pl.multiple_of(y_lo * 4 * ROWS, 4 * ROWS), 4 * ROWS)], w_in, load_sem.at[0]
    )
    load_w.start()
    load_c = pltpu.make_async_copy(cotangent, cot.at[0], load_sem.at[1])
    load_c.start()
    for s in range(SLOTS):
        pltpu.make_async_copy(hidden.at[:, hid_cols(s, core)], hid.at[s, 0], load_sem.at[2 + s]).start()

    barrier = pltpu.get_barrier_semaphore()
    pl.semaphore_signal(barrier, inc=1, device_id=partner, device_id_type=MESH)
    for axis in AXES:
        for j in (1, 2, 3):
            pl.semaphore_signal(barrier, inc=1, device_id=device(moved(at, axis, j), core), device_id_type=MESH)

    load_w.wait()
    lim = jnp.full((1, WIDTH), limit[0], f32)
    scale = 448.0 / lim

    def quantize(w, cols):
        return jnp.clip(w.astype(f32) * scale[:, cols], -448.0, 448.0).astype(bf16)

    split = GATHER[2][0]
    for z in range(4):
        codes[at["x"], at["y"], z, :, :split] = quantize(w_in[z * ROWS : (z + 1) * ROWS, :split], slice(0, split))
    own_rows = w_in[pl.ds(pl.multiple_of(at["z"] * ROWS, ROWS), ROWS), :]
    codes[at["x"], at["y"], at["z"], :, split:] = quantize(own_rows[:, split:], slice(split, WIDTH))

    pl.semaphore_wait(barrier, 10)

    def view(ref, where, rows, cols):
        return ref.at[where["x"], where["y"], where["z"], rows, cols]

    def gather_direct(k, phase):
        first, size, order = GATHER[k]
        where = dict(at)
        for axis in order[:phase]:
            where[axis] = whole()
        src = view(codes, where, slice(None), pl.ds(first, size))
        return [
            remote(src, src, ag_send.at[k, phase * 3 + j - 1], ag_recv.at[k, phase * 3 + j - 1],
                   device(moved(at, order[phase], j), core))
            for j in (1, 2, 3)
        ]

    ag_first = gather_direct(2, 0)
    start(ag_first)
    ag_mid = [gather_direct(0, 1), gather_direct(1, 1), gather_direct(2, 1)]
    start(ag_mid[0] + ag_mid[1])

    swaps = [remote(cotangent, cot.at[1], swap_send.at[0], swap_recv.at[0], partner)]
    for s in range(SLOTS):
        swaps.append(
            remote(hidden.at[:, hid_cols(s, other)], hid.at[s, 1], swap_send.at[1 + s], swap_recv.at[1 + s], partner)
        )
    start(swaps)

    peak[0] = jnp.max(
        jnp.abs(own_rows.astype(f32)).reshape(ROWS // 8, 8, WIDTH // 128, 128).max(axis=0), axis=1
    )

    def peak_phase(p):
        targets = [partner] if p == 3 else [device(moved(at, AXES[p], j), core) for j in (1, 2, 3)]
        copies = [
            remote(peak.at[p], peak_in.at[p, j], peak_send.at[p, j], peak_recv.at[p, j], to)
            for j, to in enumerate(targets)
        ]
        start(copies)
        return copies

    def peak_join(p, copies):
        best = peak[p]
        for j, copy in enumerate(copies):
            copy.wait_recv()
            best = jnp.maximum(best, peak_in[p, j])
        peak[p + 1] = best

    peaks = peak_phase(0)

    for copy in ag_first:
        copy.wait_recv()
    start(ag_mid[2])

    def partials(first, size, arrive):
        @pl.loop(0, SLOTS)
        def _(s):
            if arrive:
                pltpu.make_async_copy(hidden.at[:, hid_cols(0, core)], hid.at[s, 0], load_sem.at[2 + s]).wait()
                remote(
                    hidden.at[:, hid_cols(0, other)], hid.at[s, 1], swap_send.at[1 + s], swap_recv.at[1 + s], partner
                ).wait_recv()
            term = lax.dot_general(
                hid[s].reshape(2 * TOK, BLOCK), cot[:, :, first : first + size].reshape(2 * TOK, size),
                (((0,), (0,)), ((), ())), preferred_element_type=f32,
            )
            partial[s // 2, pl.ds(lax.rem(s, 2) * 2, 2), :, :, first : first + size] = term.astype(bf16).reshape(
                2, 4, ROWS, size
            )

    def ring(k, n, by, half, slot):
        rows, first, size, order = REDUCE[k]
        where = {order[0]: lax.rem(at[order[0]] + by, 4), order[1]: pl.ds(2 * half, 2), order[2]: whole()}
        to = device(moved(at, order[0], 1 if n % 2 == 0 else 3), core)
        return remote(
            view(partial, where, half_rows(rows), pl.ds(first, size)), first_in[k].at[slot],
            rs_send.at[k, n], rs_recv.at[k, n], to,
        )

    rs_ring = [
        [ring(k, 0, 2, 0, 0), ring(k, 1, 2, 1, 1), ring(k, 2, 1, 1, 2), ring(k, 3, 3, 0, 3),
         ring(k, 4, 1, 0, 4), ring(k, 5, 3, 1, 5)]
        for k in range(GROUPS)
    ]

    def ring_begin(groups):
        for k in groups:
            start(rs_ring[k][0:2])
        for k in groups:
            start(rs_ring[k][2:4])

    def part(k, by, half, a, b):
        rows, first, size, order = REDUCE[k]
        where = {order[0]: lax.rem(at[order[0]] + by, 4), order[1]: 2 * half + a, order[2]: b}
        return (where["x"], where["y"], where["z"], half_rows(rows), pl.ds(first, size))

    def add_landed(k, by, half, slots):
        @pl.loop(0, 4)
        def _(b):
            for a in (0, 1):
                index = part(k, by, half, a, b)
                acc = partial[index].astype(f32)
                for slot in slots:
                    acc += first_in[k][spot(k, slot, a, b)].astype(f32)
                partial[index] = acc.astype(bf16)

    def ring_forward(k):
        for n, by, half in ((0, 1, 0), (1, 3, 1)):
            rs_ring[k][n].wait_recv()
            add_landed(k, by, half, (n,))
            start([rs_ring[k][4 + n]])

    def reduce_direct(k, phase):
        rows, first, size, order = REDUCE[k]
        landing = second_in if phase == 1 else third_in
        copies = []
        for j in (1, 2, 3):
            where = {order[0]: at[order[0]], order[1]: at[order[1]], order[2]: whole()}
            where[order[phase]] = lax.rem(at[order[phase]] + j, 4)
            n = 6 + (phase - 1) * 3 + j - 1
            copies.append(
                remote(view(partial, where, half_rows(rows), pl.ds(first, size)), landing[k].at[j - 1],
                       rs_send.at[k, n], rs_recv.at[k, n], device(moved(at, order[phase], j), core))
            )
        return copies

    rs_second = [reduce_direct(k, 1) for k in range(GROUPS)]
    rs_third = [reduce_direct(k, 2) for k in range(GROUPS)]

    def ring_end(k):
        for n in range(2, 6):
            rs_ring[k][n].wait_recv()
        add_landed(k, 0, 0, (3, 4))
        add_landed(k, 0, 1, (2, 5))
        start(rs_second[k])

    def second_end(k):
        rows, first, size, order = REDUCE[k]
        for copy in rs_second[k]:
            copy.wait_recv()

        @pl.loop(0, 4)
        def _(b):
            where = {order[0]: at[order[0]], order[1]: at[order[1]], order[2]: b}
            index = (where["x"], where["y"], where["z"], half_rows(rows), pl.ds(first, size))
            acc = partial[index].astype(f32)
            for j in range(3):
                acc += second_in[k][j, b].astype(f32)
            partial[index] = acc.astype(bf16)

        start(rs_third[k])

    def piece(half, lo, z):
        return pl.ds(pl.multiple_of((lo * 4 + z) * ROWS + half * HALF, HALF), HALF)

    def third_end(k):
        rows, first, size, order = REDUCE[k]
        for copy in rs_third[k]:
            copy.wait_recv()
        acc = partial[at["x"], at["y"], at["z"], half_rows(rows), pl.ds(first, size)].astype(f32)
        for j in range(3):
            acc += third_in[k][j].astype(f32)
        wgrad_out[piece(rows, y_lo, at["z"]), pl.ds(first, size)] = (acc * (32768.0**-0.5)).astype(bf16)

    beside = device({**at, "y": at["y"] + 1 - 2 * y_lo}, core)

    def spread(half, n, rows, to):
        src = wgrad_out.at[rows]
        return remote(src, src, rep_send.at[half, n], rep_recv.at[half, n], to)

    near = [device(moved(at, "z", j), core) for j in (1, 3, 2)]
    rep = []
    for half in (0, 1):
        mine, across = piece(half, y_lo, at["z"]), piece(half, 1 - y_lo, at["z"])
        far = piece(half, y_lo, lax.rem(at["z"] + 2, 4))
        rep.append(
            [spread(half, 0, mine, beside)]
            + [spread(half, 1 + n, mine, to) for n, to in enumerate(near)]
            + [spread(half, 4, across, near[0]), spread(half, 5, across, near[1]), spread(half, 6, far, beside)]
        )

    def spread_more(half):
        rep[half][0].wait_recv()
        start(rep[half][4:6])
        rep[half][3].wait_recv()
        start(rep[half][6:7])

    def gather_ring(k, n, by, half):
        first, size, order = GATHER[k]
        where = {axis: whole() for axis in AXES}
        where[order[2]] = lax.rem(at[order[2]] + by, 4)
        where[order[0]] = pl.ds(2 * half, 2)
        src = view(codes, where, slice(None), pl.ds(first, size))
        to = device(moved(at, order[2], 1 if n % 2 == 0 else 3), core)
        return remote(src, src, ag_send.at[k, 6 + n], ag_recv.at[k, 6 + n], to)

    ag_ring = [
        [gather_ring(k, 0, 0, 0), gather_ring(k, 1, 0, 1), gather_ring(k, 2, 0, 1), gather_ring(k, 3, 0, 0),
         gather_ring(k, 4, 3, 0), gather_ring(k, 5, 1, 1)]
        for k in range(3)
    ]

    def gather_last(k):
        for copy in ag_mid[k]:
            copy.wait_recv()
        start(ag_ring[k][:4])

    def gather_forward(k):
        for n in (0, 1):
            ag_ring[k][n].wait_recv()
            start([ag_ring[k][4 + n]])

    unscale = limit[0] * (1.0 / 448.0)

    def matmuls(lo, hi):
        @pl.loop(lo, hi)
        def _(s):
            w_s = codes[s // 2, pl.ds(lax.rem(s, 2) * 2, 2)].reshape(BLOCK, WIDTH)
            h = hid[s].reshape(2 * TOK, BLOCK)
            for n in range(0, WIDTH, 512):
                keys_acc[:, n : n + 512] += jnp.dot(h, w_s[:, n : n + 512], preferred_element_type=f32)
            c_all = cot[...].reshape(2 * TOK, WIDTH)
            for n in range(0, BLOCK, 256):
                g = lax.dot_general(c_all, w_s[n : n + 256], (((1,), (1,)), ((), ())), preferred_element_type=f32)
                g = (g * unscale).astype(bf16)
                grad_stage[s, :, n : n + 256] = g[TOK:]
                grad_out[:, pl.ds(pl.multiple_of((s * 2 + core) * BLOCK + n, 256), 256)] = g[:TOK]
            remote(
                grad_stage.at[s], grad_out.at[:, hid_cols(s, core)], grad_send.at[s], grad_recv.at[s], partner
            ).start()

    load_c.wait()
    swaps[0].wait_recv()
    partials(512, 512, True)
    ring_begin((0, 3))
    partials(0, 512, False)
    ring_begin((1, 2))
    ring_begin((4, 5))
    peak_join(0, peaks)
    peaks = peak_phase(1)
    for k in range(3):
        gather_last(k)
    keys_acc[...] = jnp.zeros_like(keys_acc)
    for k in range(GROUPS):
        ring_forward(k)
    peak_join(1, peaks)
    peaks = peak_phase(2)
    for k in range(3):
        gather_forward(k)
    for k in range(GROUPS):
        ring_end(k)
    peak_join(2, peaks)
    peaks = peak_phase(3)
    for k in range(3):
        for copy in ag_ring[k][2:]:
            copy.wait_recv()
    matmuls(0, 2)
    for k in (0, 1, 2):
        second_end(k)
    matmuls(2, 4)
    for k in (3, 4, 5):
        second_end(k)
    matmuls(4, 6)
    for k in (0, 1, 2):
        third_end(k)
    start(rep[0][:4])
    matmuls(6, 8)
    for k in (3, 4, 5):
        third_end(k)
    start(rep[1][:4])
    keys_send[...] = keys_acc[TOK:].astype(bf16)
    key_copy = remote(keys_send, keys_recv, key_send.at[0], key_recv.at[0], partner)
    start([key_copy])
    spread_more(0)
    peak_join(3, peaks)
    ratio_out[0] = jnp.max(peak[4] / jnp.full((8, 128), limit[0], f32))
    key_copy.wait_recv()
    keys_out[...] = ((keys_acc[:TOK] + keys_recv[...].astype(f32)) * unscale).astype(bf16)
    spread_more(1)

    for s in range(SLOTS):
        remote(grad_stage.at[s], grad_out.at[:, hid_cols(s, core)], grad_send.at[s], grad_recv.at[s], partner).wait()
    for half in (0, 1):
        for n in (1, 2, 4, 5, 6):
            rep[half][n].wait_recv()
    for copy in sent:
        copy.wait_send()


def place(keys, grad, wgrad, keys_out, grad_out, wgrad_out, sem):
    copies = [
        pltpu.make_async_copy(src, dst, sem.at[n])
        for n, (src, dst) in enumerate(((grad, grad_out), (wgrad, wgrad_out), (keys, keys_out)))
    ]
    for copy in copies:
        copy.start()
    for copy in copies:
        copy.wait()


def landing(k, phase):
    size = REDUCE[k][2]
    shape = (spot(k, 6, 2, 4), (3, 4), (3,))[phase]
    return pltpu.VMEM((*shape, HALF, size), jnp.bfloat16)


def body(hidden_states, key_weight, previous_peak, key_cotangent):
    bf16, f32 = jnp.bfloat16, jnp.float32
    any_space = pl.BlockSpec(memory_space=pl.ANY)
    hbm = pl.BlockSpec(memory_space=pltpu.HBM)
    vmem = pl.BlockSpec(memory_space=pltpu.VMEM)
    smem = pl.BlockSpec(memory_space=pltpu.SMEM)
    dma = pltpu.SemaphoreType.DMA
    shapes = ((TOK, WIDTH), (TOK, 2 * SLOTS * BLOCK), (BLOCK, WIDTH))
    *results, ratio = pl.pallas_call(
        kernel,
        out_shape=(*[pltpu.VMEM(shape, bf16) for shape in shapes], jax.ShapeDtypeStruct((1,), f32)),
        in_specs=[hbm, hbm, smem, hbm],
        out_specs=(vmem, vmem, vmem, smem),
        scratch_shapes=[
            pltpu.VMEM((4 * ROWS, WIDTH), bf16),
            pltpu.VMEM((4, 4, 4, ROWS, WIDTH), bf16),
            pltpu.VMEM((4, 4, 4, ROWS, WIDTH), bf16),
            pltpu.VMEM((SLOTS, 2, TOK, BLOCK), bf16),
            pltpu.VMEM((2, TOK, WIDTH), bf16),
            pltpu.VMEM((2 * TOK, WIDTH), f32),
            pltpu.VMEM((TOK, WIDTH), bf16),
            pltpu.VMEM((TOK, WIDTH), bf16),
            pltpu.VMEM((SLOTS, TOK, BLOCK), bf16),
            pltpu.VMEM((5, 8, 128), f32),
            pltpu.VMEM((4, 3, 8, 128), f32),
            *[landing(k, phase) for phase in range(3) for k in range(GROUPS)],
            dma((2 + SLOTS,)),
            dma((1 + SLOTS,)),
            dma((1 + SLOTS,)),
            dma((3, 12)),
            dma((3, 12)),
            dma((GROUPS, 12)),
            dma((GROUPS, 12)),
            dma((2, 7)),
            dma((2, 7)),
            dma((4, 3)),
            dma((4, 3)),
            dma((1,)),
            dma((1,)),
            dma((SLOTS,)),
            dma((SLOTS,)),
        ],
        compiler_params=pltpu.CompilerParams(
            collective_id=0, has_side_effects=True, vmem_limit_bytes=44 * 2**20
        ),
    )(
        pltpu.with_memory_space_constraint(hidden_states, pltpu.HBM),
        pltpu.with_memory_space_constraint(key_weight, pltpu.HBM),
        previous_peak,
        pltpu.with_memory_space_constraint(key_cotangent, pltpu.HBM),
    )
    keys, grad, wgrad = pl.pallas_call(
        place,
        out_shape=tuple(jax.ShapeDtypeStruct(shape, bf16) for shape in shapes),
        in_specs=[any_space] * 3,
        out_specs=(any_space,) * 3,
        scratch_shapes=[dma((3,))],
        compiler_params=pltpu.CompilerParams(vmem_limit_bytes=2**20),
    )(*[pltpu.with_memory_space_constraint(array, pltpu.VMEM) for array in results])
    return keys, grad, wgrad, ratio


def solution(mesh):
    in_specs = (P(("replica", "fsdp"), None), P("fsdp", None), P(), P(("replica", "fsdp"), None))
    out_specs = (P(("replica", "fsdp"), None), P(("replica", "fsdp"), None), P("fsdp", None), P())
    return jax.shard_map(body, mesh=mesh, in_specs=in_specs, out_specs=out_specs, check_vma=False)
```

```python
import jax
import jax.numpy as jnp
from jax import lax
from jax.experimental import pallas as pl
from jax.experimental.pallas import tpu as pltpu
from jax.sharding import PartitionSpec as P

MESH = pl.DeviceIdType.MESH
AXES = ("x", "y", "z")
ROWS = 64
WIDTH = 1024
TOK = 256
SLOTS = 8
BLOCK = 512
GATHER = (
    (0, 384, ("z", "y", "x")),
    (384, 256, ("x", "z", "y")),
    (640, 384, ("y", "x", "z")),
)
REDUCE = (
    (0, 640, 384, ("z", "y", "x")),
    (0, 0, 384, ("x", "y", "z")),
    (0, 384, 256, ("y", "x", "z")),
    (1, 640, 384, ("z", "y", "x")),
    (1, 0, 256, ("x", "y", "z")),
    (1, 256, 384, ("y", "x", "z")),
)
SCHEDULE = (
    ("gather_first", 2), ("gather_first", 1), ("swap", 0), ("peak", 0), ("gather_second", 0), ("gather_second", 1),
    ("gather_second", 2), ("partials", 0), ("peak", 1), ("ring_far", 0), ("gather_near", 1), ("ring_far", 3),
    ("gather_near", 0), ("partials", 1), ("peak", 2), ("ring_near", 1), ("ring_near", 0), ("gather_near", 2),
    ("ring_far", 1), ("ring_near", 4), ("ring_near", 3), ("gather_rest", 1), ("ring_far", 5), ("ring_near", 5),
    ("ring_sum", 0), ("ring_far", 2), ("ring_sum", 1), ("gather_rest", 0), ("ring_sum", 3), ("ring_near", 2),
    ("ring_sum", 2), ("ring_sum", 5), ("second_axis", 1), ("gather_far", 2), ("ring_far", 4), ("second_axis", 2),
    ("second_axis", 0), ("second_axis", 3), ("gather_rest", 2), ("ring_sum", 4), ("third_axis", 2),
    ("second_axis", 5), ("third_axis", 0), ("second_axis", 4), ("third_axis", 1), ("gather_far", 1),
    ("third_axis", 3), ("third_axis", 5), ("gather_far", 0), ("third_axis", 4), ("matmuls", 0), ("peak", 3),
    ("matmuls", 1), ("spread", 0), ("matmuls", 2), ("matmuls", 3), ("spread", 1), ("matmuls", 4), ("matmuls", 5),
    ("matmuls", 6), ("spread_more", 0), ("matmuls", 7), ("spread_more", 1), ("spread_end", 1), ("keys", 0),
    ("spread_end", 0), ("peak", 4),
)
GROUPS = len(REDUCE)
HALF = ROWS // 2


def position():
    replica, fsdp = lax.axis_index("replica"), lax.axis_index("fsdp")
    y_lo, z = replica // 4, lax.rem(replica, 4)
    x, y_hi, core = fsdp // 4, lax.rem(fsdp // 2, 2), lax.rem(fsdp, 2)
    return {"x": x, "y": y_hi * 2 + y_lo, "z": z}, core


def device(at, core):
    y_hi, y_lo = at["y"] // 2, lax.rem(at["y"], 2)
    return (y_lo * 4 + at["z"], at["x"] * 4 + y_hi * 2 + core)


def moved(at, axis, by):
    return {**at, axis: lax.rem(at[axis] + by, 4)}


def whole():
    return pl.ds(0, 4)


def spot(k, slot, a, b):
    order = REDUCE[k][3]
    return (slot, a, b) if AXES.index(order[1]) < AXES.index(order[2]) else (slot, b, a)


def half_rows(half):
    return pl.ds(half * HALF, HALF)


def kernel(hidden, weight, limit, cotangent, keys_out, grad_out, wgrad_out, ratio_out, *scratch):
    (w_in, codes, partial, hid, cot, keys_acc, keys_send, keys_recv, grad_stage, peak, peak_in) = scratch[:11]
    landings = scratch[11 : 11 + 3 * GROUPS]
    first_in, second_in, third_in = (landings[n * GROUPS : (n + 1) * GROUPS] for n in range(3))
    (load_sem, swap_send, swap_recv, ag_send, ag_recv, rs_send, rs_recv, rep_send, rep_recv,
     peak_send, peak_recv, key_send, key_recv, grad_send, grad_recv) = scratch[11 + 3 * GROUPS :]

    at, core = position()
    other = 1 - core
    partner = device(at, other)
    f32, bf16 = jnp.float32, jnp.bfloat16
    y_lo = lax.rem(at["y"], 2)

    def remote(src, dst, send, recv, to):
        return pltpu.make_async_remote_copy(
            src_ref=src, dst_ref=dst, send_sem=send, recv_sem=recv, device_id=to, device_id_type=MESH
        )

    sent, landed = [], set()

    def start(copies):
        for copy in copies:
            copy.start()
            sent.append(copy)

    def arrive(copies):
        for copy in copies:
            if id(copy) not in landed:
                landed.add(id(copy))
                copy.wait_recv()

    def hid_cols(slot, which):
        return pl.ds(pl.multiple_of((slot * 2 + which) * BLOCK, BLOCK), BLOCK)

    load_w = pltpu.make_async_copy(
        weight.at[pl.ds(pl.multiple_of(y_lo * 4 * ROWS, 4 * ROWS), 4 * ROWS)], w_in, load_sem.at[0]
    )
    load_w.start()
    load_c = pltpu.make_async_copy(cotangent, cot.at[0], load_sem.at[1])
    load_c.start()
    for s in range(SLOTS):
        pltpu.make_async_copy(hidden.at[:, hid_cols(s, core)], hid.at[s, 0], load_sem.at[2 + s]).start()

    barrier = pltpu.get_barrier_semaphore()
    pl.semaphore_signal(barrier, inc=1, device_id=partner, device_id_type=MESH)
    for axis in AXES:
        for j in (1, 2, 3):
            pl.semaphore_signal(barrier, inc=1, device_id=device(moved(at, axis, j), core), device_id_type=MESH)

    load_w.wait()
    lim = jnp.full((1, WIDTH), limit[0], f32)
    scale = 448.0 / lim

    def quantize(w, first, size):
        return jnp.clip(w.astype(f32) * scale[:, first : first + size], -448.0, 448.0).astype(bf16)

    own_rows = w_in[pl.ds(pl.multiple_of(at["z"] * ROWS, ROWS), ROWS), :]
    for first, size, order in GATHER:
        if order[0] == "z":
            for z in range(4):
                line = w_in[z * ROWS : (z + 1) * ROWS, first : first + size]
                codes[at["x"], at["y"], z, :, first : first + size] = quantize(line, first, size)
        else:
            mine = own_rows[:, first : first + size]
            codes[at["x"], at["y"], at["z"], :, first : first + size] = quantize(mine, first, size)

    pl.semaphore_wait(barrier, 10)

    def view(ref, where, rows, cols):
        return ref.at[where["x"], where["y"], where["z"], rows, cols]

    def gather_direct(k, phase):
        first, size, order = GATHER[k]
        where = dict(at)
        for axis in order[:phase]:
            where[axis] = whole()
        src = view(codes, where, slice(None), pl.ds(first, size))
        return [
            remote(src, src, ag_send.at[k, phase * 3 + j - 1], ag_recv.at[k, phase * 3 + j - 1],
                   device(moved(at, order[phase], j), core))
            for j in (1, 2, 3)
        ]

    ag_first = [[] if order[0] == "z" else gather_direct(k, 0) for k, (_, _, order) in enumerate(GATHER)]
    ag_mid = [gather_direct(k, 1) for k in range(3)]

    swaps = [remote(cotangent, cot.at[1], swap_send.at[0], swap_recv.at[0], partner)]
    for s in range(SLOTS):
        swaps.append(
            remote(hidden.at[:, hid_cols(s, other)], hid.at[s, 1], swap_send.at[1 + s], swap_recv.at[1 + s], partner)
        )

    peak[0] = jnp.max(
        jnp.abs(own_rows.astype(f32)).reshape(ROWS // 8, 8, WIDTH // 128, 128).max(axis=0), axis=1
    )

    peaks = {}

    def peak_phase(p):
        targets = [partner] if p == 3 else [device(moved(at, AXES[p], j), core) for j in (1, 2, 3)]
        copies = [
            remote(peak.at[p], peak_in.at[p, j], peak_send.at[p, j], peak_recv.at[p, j], to)
            for j, to in enumerate(targets)
        ]
        start(copies)
        peaks[p] = copies

    def peak_join(p):
        best = peak[p]
        for j, copy in enumerate(peaks[p]):
            copy.wait_recv()
            best = jnp.maximum(best, peak_in[p, j])
        peak[p + 1] = best

    def partials(first, size, arrive):
        @pl.loop(0, SLOTS)
        def _(s):
            if arrive:
                pltpu.make_async_copy(hidden.at[:, hid_cols(0, core)], hid.at[s, 0], load_sem.at[2 + s]).wait()
                remote(
                    hidden.at[:, hid_cols(0, other)], hid.at[s, 1], swap_send.at[1 + s], swap_recv.at[1 + s], partner
                ).wait_recv()
            term = lax.dot_general(
                hid[s].reshape(2 * TOK, BLOCK), cot[:, :, first : first + size].reshape(2 * TOK, size),
                (((0,), (0,)), ((), ())), preferred_element_type=f32,
            )
            partial[s // 2, pl.ds(lax.rem(s, 2) * 2, 2), :, :, first : first + size] = term.astype(bf16).reshape(
                2, 4, ROWS, size
            )

    def ring(k, n, by, half, slot):
        rows, first, size, order = REDUCE[k]
        where = {order[0]: lax.rem(at[order[0]] + by, 4), order[1]: pl.ds(2 * half, 2), order[2]: whole()}
        to = device(moved(at, order[0], 1 if n % 2 == 0 else 3), core)
        return remote(
            view(partial, where, half_rows(rows), pl.ds(first, size)), first_in[k].at[slot],
            rs_send.at[k, n], rs_recv.at[k, n], to,
        )

    rs_ring = [
        [ring(k, 0, 2, 0, 0), ring(k, 1, 2, 1, 1), ring(k, 2, 1, 1, 2), ring(k, 3, 3, 0, 3),
         ring(k, 4, 1, 0, 4), ring(k, 5, 3, 1, 5)]
        for k in range(GROUPS)
    ]

    def part(k, by, half, a, b):
        rows, first, size, order = REDUCE[k]
        where = {order[0]: lax.rem(at[order[0]] + by, 4), order[1]: 2 * half + a, order[2]: b}
        return (where["x"], where["y"], where["z"], half_rows(rows), pl.ds(first, size))

    def add_landed(k, by, half, slots):
        @pl.loop(0, 4)
        def _(b):
            for a in (0, 1):
                index = part(k, by, half, a, b)
                acc = partial[index].astype(f32)
                for slot in slots:
                    acc += first_in[k][spot(k, slot, a, b)].astype(f32)
                partial[index] = acc.astype(bf16)

    def ring_forward(k):
        for n, by, half in ((0, 1, 0), (1, 3, 1)):
            arrive([rs_ring[k][n]])
            add_landed(k, by, half, (n,))
            start([rs_ring[k][4 + n]])

    def reduce_direct(k, phase):
        rows, first, size, order = REDUCE[k]
        landing = second_in if phase == 1 else third_in
        copies = []
        for j in (1, 2, 3):
            where = {order[0]: at[order[0]], order[1]: at[order[1]], order[2]: whole()}
            where[order[phase]] = lax.rem(at[order[phase]] + j, 4)
            n = 6 + (phase - 1) * 3 + j - 1
            copies.append(
                remote(view(partial, where, half_rows(rows), pl.ds(first, size)), landing[k].at[j - 1],
                       rs_send.at[k, n], rs_recv.at[k, n], device(moved(at, order[phase], j), core))
            )
        return copies

    rs_second = [reduce_direct(k, 1) for k in range(GROUPS)]
    rs_third = [reduce_direct(k, 2) for k in range(GROUPS)]

    def ring_end(k):
        arrive(rs_ring[k][2:])
        add_landed(k, 0, 0, (3, 4))
        add_landed(k, 0, 1, (2, 5))
        start(rs_second[k])

    def second_end(k):
        rows, first, size, order = REDUCE[k]
        arrive(rs_second[k])

        @pl.loop(0, 4)
        def _(b):
            where = {order[0]: at[order[0]], order[1]: at[order[1]], order[2]: b}
            index = (where["x"], where["y"], where["z"], half_rows(rows), pl.ds(first, size))
            acc = partial[index].astype(f32)
            for j in range(3):
                acc += second_in[k][j, b].astype(f32)
            partial[index] = acc.astype(bf16)

        start(rs_third[k])

    def piece(half, lo, z):
        return pl.ds(pl.multiple_of((lo * 4 + z) * ROWS + half * HALF, HALF), HALF)

    def third_end(k):
        rows, first, size, order = REDUCE[k]
        arrive(rs_third[k])
        acc = partial[at["x"], at["y"], at["z"], half_rows(rows), pl.ds(first, size)].astype(f32)
        for j in range(3):
            acc += third_in[k][j].astype(f32)
        wgrad_out[piece(rows, y_lo, at["z"]), pl.ds(first, size)] = (acc * (32768.0**-0.5)).astype(bf16)

    beside = device({**at, "y": at["y"] + 1 - 2 * y_lo}, core)

    def spread(half, n, rows, to):
        src = wgrad_out.at[rows]
        return remote(src, src, rep_send.at[half, n], rep_recv.at[half, n], to)

    near = [device(moved(at, "z", j), core) for j in (1, 3, 2)]
    rep = []
    for half in (0, 1):
        mine, across = piece(half, y_lo, at["z"]), piece(half, 1 - y_lo, at["z"])
        far = piece(half, y_lo, lax.rem(at["z"] + 2, 4))
        rep.append(
            [spread(half, 0, mine, beside)]
            + [spread(half, 1 + n, mine, to) for n, to in enumerate(near)]
            + [spread(half, 4, across, near[0]), spread(half, 5, across, near[1]), spread(half, 6, far, beside)]
        )

    def spread_more(half):
        arrive(rep[half][:1])
        start(rep[half][4:6])
        arrive(rep[half][3:4])
        start(rep[half][6:7])

    def gather_ring(k, n, by, half):
        first, size, order = GATHER[k]
        where = {axis: whole() for axis in AXES}
        where[order[2]] = lax.rem(at[order[2]] + by, 4)
        where[order[0]] = pl.ds(2 * half, 2)
        src = view(codes, where, slice(None), pl.ds(first, size))
        to = device(moved(at, order[2], 1 if n % 2 == 0 else 3), core)
        return remote(src, src, ag_send.at[k, 6 + n], ag_recv.at[k, 6 + n], to)

    ag_ring = [
        [gather_ring(k, 0, 0, 0), gather_ring(k, 1, 0, 1), gather_ring(k, 2, 0, 1), gather_ring(k, 3, 0, 0),
         gather_ring(k, 4, 3, 0), gather_ring(k, 5, 1, 1)]
        for k in range(3)
    ]

    def gather_near(k):
        arrive(ag_mid[k])
        start(ag_ring[k][:2])

    def gather_far(k):
        for n in (0, 1):
            arrive([ag_ring[k][n]])
            start([ag_ring[k][4 + n]])

    unscale = limit[0] * (1.0 / 448.0)

    last = {order[2]: k for k, (_, _, order) in enumerate(GATHER)}

    def matmuls(n):
        if n == 0:
            for k in range(3):
                arrive(ag_ring[k][:4])
            arrive(ag_ring[last["z"]][4:])
        elif n == 3:
            arrive(ag_ring[last["y"]][4:])
        elif n == 6:
            arrive(ag_ring[last["x"]][4:])
        by, across = ((0, 0), (1, 0), (3, 0), (0, 1), (1, 1), (3, 1), (2, 0), (2, 1))[n]
        x = lax.rem(at["x"] + by, 4)
        y_hi = lax.rem(at["y"] // 2 + across, 2)
        s = x * 2 + y_hi
        w_s = codes[x, pl.ds(y_hi * 2, 2)].reshape(BLOCK, WIDTH)
        h = hid[s].reshape(2 * TOK, BLOCK)
        for c in range(0, WIDTH, 512):
            term = jnp.dot(h, w_s[:, c : c + 512], preferred_element_type=f32)
            keys_acc[:, c : c + 512] = term if n == 0 else keys_acc[:, c : c + 512] + term
        c_all = cot[...].reshape(2 * TOK, WIDTH)
        for c in range(0, BLOCK, 256):
            g = lax.dot_general(c_all, w_s[c : c + 256], (((1,), (1,)), ((), ())), preferred_element_type=f32)
            g = (g * unscale).astype(bf16)
            grad_stage[s, :, c : c + 256] = g[TOK:]
            grad_out[:, pl.ds(pl.multiple_of((s * 2 + core) * BLOCK + c, 256), 256)] = g[:TOK]
        remote(
            grad_stage.at[s], grad_out.at[:, hid_cols(s, core)], grad_send.at[s], grad_recv.at[s], partner
        ).start()
        if n == SLOTS - 1:
            keys_send[...] = keys_acc[TOK:].astype(bf16)
            start([key_copy])

    key_copy = remote(keys_send, keys_recv, key_send.at[0], key_recv.at[0], partner)

    def step(name, n):
        if name == "gather_first":
            start(ag_first[n])
        elif name == "gather_second":
            arrive(ag_first[n])
            start(ag_mid[n])
        elif name == "gather_near":
            gather_near(n)
        elif name == "gather_rest":
            start(ag_ring[n][2:4])
        elif name == "gather_far":
            gather_far(n)
        elif name == "swap":
            start(swaps)
        elif name == "partials":
            if n == 0:
                load_c.wait()
                arrive(swaps[:1])
            partials(512 - 512 * n, 512, n == 0)
        elif name == "ring_far":
            start(rs_ring[n][:2])
        elif name == "ring_near":
            start(rs_ring[n][2:4])
        elif name == "ring_sum":
            ring_forward(n)
        elif name == "second_axis":
            ring_end(n)
        elif name == "third_axis":
            second_end(n)
        elif name == "spread":
            for k in range(3 * n, 3 * n + 3):
                third_end(k)
            start(rep[n][:4])
        elif name == "spread_more":
            spread_more(n)
        elif name == "spread_end":
            arrive(rep[n])
        elif name == "matmuls":
            matmuls(n)
        elif name == "keys":
            arrive([key_copy])
            keys_out[...] = ((keys_acc[:TOK] + keys_recv[...].astype(f32)) * unscale).astype(bf16)
        elif name == "peak":
            if n > 0:
                peak_join(n - 1)
            if n < 4:
                peak_phase(n)
            else:
                ratio_out[0] = jnp.max(peak[4] / jnp.full((8, 128), limit[0], f32))
        else:
            raise ValueError(name)

    for name, n in SCHEDULE:
        step(name, n)

    for s in range(SLOTS):
        remote(grad_stage.at[s], grad_out.at[:, hid_cols(s, core)], grad_send.at[s], grad_recv.at[s], partner).wait()
    for copy in sent:
        copy.wait_send()


def place(keys, grad, wgrad, keys_out, grad_out, wgrad_out, sem):
    copies = [
        pltpu.make_async_copy(src, dst, sem.at[n])
        for n, (src, dst) in enumerate(((grad, grad_out), (wgrad, wgrad_out), (keys, keys_out)))
    ]
    for copy in copies:
        copy.start()
    for copy in copies:
        copy.wait()


def landing(k, phase):
    size = REDUCE[k][2]
    shape = (spot(k, 6, 2, 4), (3, 4), (3,))[phase]
    return pltpu.VMEM((*shape, HALF, size), jnp.bfloat16)


def body(hidden_states, key_weight, previous_peak, key_cotangent):
    bf16, f32 = jnp.bfloat16, jnp.float32
    any_space = pl.BlockSpec(memory_space=pl.ANY)
    hbm = pl.BlockSpec(memory_space=pltpu.HBM)
    vmem = pl.BlockSpec(memory_space=pltpu.VMEM)
    smem = pl.BlockSpec(memory_space=pltpu.SMEM)
    dma = pltpu.SemaphoreType.DMA
    shapes = ((TOK, WIDTH), (TOK, 2 * SLOTS * BLOCK), (BLOCK, WIDTH))
    *results, ratio = pl.pallas_call(
        kernel,
        out_shape=(*[pltpu.VMEM(shape, bf16) for shape in shapes], jax.ShapeDtypeStruct((1,), f32)),
        in_specs=[hbm, hbm, smem, hbm],
        out_specs=(vmem, vmem, vmem, smem),
        scratch_shapes=[
            pltpu.VMEM((4 * ROWS, WIDTH), bf16),
            pltpu.VMEM((4, 4, 4, ROWS, WIDTH), bf16),
            pltpu.VMEM((4, 4, 4, ROWS, WIDTH), bf16),
            pltpu.VMEM((SLOTS, 2, TOK, BLOCK), bf16),
            pltpu.VMEM((2, TOK, WIDTH), bf16),
            pltpu.VMEM((2 * TOK, WIDTH), f32),
            pltpu.VMEM((TOK, WIDTH), bf16),
            pltpu.VMEM((TOK, WIDTH), bf16),
            pltpu.VMEM((SLOTS, TOK, BLOCK), bf16),
            pltpu.VMEM((5, 8, 128), f32),
            pltpu.VMEM((4, 3, 8, 128), f32),
            *[landing(k, phase) for phase in range(3) for k in range(GROUPS)],
            dma((2 + SLOTS,)),
            dma((1 + SLOTS,)),
            dma((1 + SLOTS,)),
            dma((3, 12)),
            dma((3, 12)),
            dma((GROUPS, 12)),
            dma((GROUPS, 12)),
            dma((2, 7)),
            dma((2, 7)),
            dma((4, 3)),
            dma((4, 3)),
            dma((1,)),
            dma((1,)),
            dma((SLOTS,)),
            dma((SLOTS,)),
        ],
        compiler_params=pltpu.CompilerParams(
            collective_id=0, has_side_effects=True, vmem_limit_bytes=44 * 2**20
        ),
    )(
        pltpu.with_memory_space_constraint(hidden_states, pltpu.HBM),
        pltpu.with_memory_space_constraint(key_weight, pltpu.HBM),
        previous_peak,
        pltpu.with_memory_space_constraint(key_cotangent, pltpu.HBM),
    )
    keys, grad, wgrad = pl.pallas_call(
        place,
        out_shape=tuple(jax.ShapeDtypeStruct(shape, bf16) for shape in shapes),
        in_specs=[any_space] * 3,
        out_specs=(any_space,) * 3,
        scratch_shapes=[dma((3,))],
        compiler_params=pltpu.CompilerParams(vmem_limit_bytes=2**20),
    )(*[pltpu.with_memory_space_constraint(array, pltpu.VMEM) for array in results])
    return keys, grad, wgrad, ratio


def solution(mesh):
    in_specs = (P(("replica", "fsdp"), None), P("fsdp", None), P(), P(("replica", "fsdp"), None))
    out_specs = (P(("replica", "fsdp"), None), P(("replica", "fsdp"), None), P("fsdp", None), P())
    return jax.shard_map(body, mesh=mesh, in_specs=in_specs, out_specs=out_specs, check_vma=False)
```

```python
import jax
import jax.numpy as jnp
from jax import lax
from jax.experimental import pallas as pl
from jax.experimental.pallas import tpu as pltpu
from jax.sharding import PartitionSpec as P

MESH = pl.DeviceIdType.MESH
AXES = ("x", "y", "z")
ROWS = 64
WIDTH = 1024
TOK = 256
SLOTS = 8
BLOCK = 512
GATHER = (
    (0, 384, ("z", "y", "x")),
    (384, 384, ("z", "x", "y")),
    (768, 256, ("x", "y", "z")),
)
REDUCE = (
    (0, 0, 384, ("z", "x", "y")),
    (0, 384, 256, ("x", "y", "z")),
    (0, 640, 384, ("y", "z", "x")),
    (1, 0, 384, ("z", "x", "y")),
    (1, 384, 384, ("x", "z", "y")),
    (1, 768, 256, ("y", "z", "x")),
)
SCHEDULE = (
    ("gather_second", 0), ("gather_second", 1), ("gather_first", 2), ("swap", 0), ("peak", 0), ("partials", 0),
    ("peak", 1), ("ring_far", 0), ("ring_far", 3), ("ring_far", 1), ("ring_far", 2), ("ring_far", 4),
    ("ring_far", 5), ("ring_sum", 1), ("ring_near", 0), ("gather_second", 2), ("ring_sum", 5), ("peak", 2),
    ("gather_near", 0), ("gather_second_far", 1), ("ring_sum", 3), ("ring_near", 5), ("ring_near", 1),
    ("ring_sum", 2), ("ring_near", 2), ("ring_near", 3), ("ring_sum", 0), ("gather_second_far", 2),
    ("second_axis", 5), ("ring_near", 4), ("gather_near", 1), ("second_axis", 2), ("second_axis", 1),
    ("ring_sum", 4), ("second_axis", 0), ("second_axis", 3), ("gather_near", 2), ("gather_rest", 1),
    ("third_axis", 5), ("gather_rest", 0), ("gather_rest", 2), ("third_axis", 2), ("third_axis", 0),
    ("gather_far", 2), ("second_axis", 4), ("gather_far", 0), ("gather_far", 1), ("third_axis", 3), ("matmuls", 0),
    ("peak", 3), ("third_axis", 1), ("matmuls", 1), ("matmuls", 2), ("third_axis", 4), ("spread", 0), ("matmuls", 3),
    ("matmuls", 4), ("spread", 1), ("matmuls", 5), ("matmuls", 6), ("spread_more", 0), ("matmuls", 7),
    ("spread_more", 1), ("keys", 0), ("spread_end", 1), ("spread_end", 0), ("peak", 4),
)
GROUPS = len(REDUCE)
PARTS = ((0, 32), (32, 32))


def position():
    replica, fsdp = lax.axis_index("replica"), lax.axis_index("fsdp")
    y_lo, z = replica // 4, lax.rem(replica, 4)
    x, y_hi, core = fsdp // 4, lax.rem(fsdp // 2, 2), lax.rem(fsdp, 2)
    return {"x": x, "y": y_hi * 2 + y_lo, "z": z}, core


def device(at, core):
    y_hi, y_lo = at["y"] // 2, lax.rem(at["y"], 2)
    return (y_lo * 4 + at["z"], at["x"] * 4 + y_hi * 2 + core)


def moved(at, axis, by):
    return {**at, axis: lax.rem(at[axis] + by, 4)}


def whole():
    return pl.ds(0, 4)


def spot(k, slot, a, b):
    order = REDUCE[k][3]
    return (slot, a, b) if AXES.index(order[1]) < AXES.index(order[2]) else (slot, b, a)


def half_rows(half):
    return pl.ds(*PARTS[half])


def kernel(hidden, weight, limit, cotangent, keys_out, grad_out, wgrad_out, ratio_out, *scratch):
    (ratio, w_in, codes, partial, hid, cot, keys_acc, keys_send, keys_recv, grad_stage, peak, peak_in) = scratch[:12]
    landings = scratch[12 : 12 + 3 * GROUPS]
    first_in, second_in, third_in = (landings[n * GROUPS : (n + 1) * GROUPS] for n in range(3))
    (load_sem, swap_send, swap_recv, ag_send, ag_recv, rs_send, rs_recv, rep_send, rep_recv,
     peak_send, peak_recv, key_send, key_recv, grad_send, grad_recv) = scratch[12 + 3 * GROUPS :]

    at, core = position()
    other = 1 - core
    partner = device(at, other)
    f32, bf16 = jnp.float32, jnp.bfloat16
    y_lo = lax.rem(at["y"], 2)

    def remote(src, dst, send, recv, to):
        return pltpu.make_async_remote_copy(
            src_ref=src, dst_ref=dst, send_sem=send, recv_sem=recv, device_id=to, device_id_type=MESH
        )

    sent, landed = [], set()

    def start(copies):
        for copy in copies:
            copy.start()
            sent.append(copy)

    def arrive(copies):
        for copy in copies:
            if id(copy) not in landed:
                landed.add(id(copy))
                copy.wait_recv()

    def hid_cols(slot, which):
        return pl.ds(pl.multiple_of((slot * 2 + which) * BLOCK, BLOCK), BLOCK)

    load_w = pltpu.make_async_copy(weight, w_in, load_sem.at[0])
    load_w.start()
    load_c = pltpu.make_async_copy(cotangent, cot.at[0], load_sem.at[1])
    load_c.start()
    for s in range(SLOTS):
        pltpu.make_async_copy(hidden.at[:, hid_cols(s, core)], hid.at[s, 0], load_sem.at[2 + s]).start()

    barrier = pltpu.get_barrier_semaphore()
    pl.semaphore_signal(barrier, inc=1, device_id=partner, device_id_type=MESH)
    for axis in AXES:
        for j in (1, 2, 3):
            pl.semaphore_signal(barrier, inc=1, device_id=device(moved(at, axis, j), core), device_id_type=MESH)

    load_w.wait()
    lim = jnp.full((1, WIDTH), limit[0], f32)
    scale = 448.0 / lim

    def quantize(w, first, size):
        return jnp.clip(w.astype(f32) * scale[:, first : first + size], -448.0, 448.0).astype(bf16)

    def rows_of(lo, z):
        return pl.ds(pl.multiple_of((lo * 4 + z) * ROWS, ROWS), ROWS)

    own_rows = w_in[rows_of(y_lo, at["z"]), :]
    pair = at["y"] - y_lo
    for first, size, order in GATHER:
        cols = slice(first, first + size)
        if order[:2] == ("z", "y"):
            block = quantize(w_in[:, cols], first, size)
            codes[at["x"], pl.ds(pair, 2), :, :, cols] = block.reshape(2, 4, ROWS, size)
        elif order[0] == "z":
            for z in range(4):
                codes[at["x"], at["y"], z, :, cols] = quantize(w_in[rows_of(y_lo, z), cols], first, size)
        else:
            codes[at["x"], at["y"], at["z"], :, cols] = quantize(own_rows[:, cols], first, size)

    pl.semaphore_wait(barrier, 10)

    def view(ref, where, rows, cols):
        return ref.at[where["x"], where["y"], where["z"], rows, cols]

    def gather_direct(k):
        first, size, order = GATHER[k]
        src = view(codes, at, slice(None), pl.ds(first, size))
        return [
            remote(src, src, ag_send.at[k, j - 1], ag_recv.at[k, j - 1], device(moved(at, order[0], j), core))
            for j in (1, 2, 3)
        ]

    def gather_ring(k, phase, n, by, half):
        first, size, order = GATHER[k]
        where = {order[0]: pl.ds(2 * half, 2), order[1]: whole(), order[2]: at[order[2]]}
        where[order[phase]] = lax.rem(at[order[phase]] + by, 4)
        src = view(codes, where, slice(None), pl.ds(first, size))
        to = device(moved(at, order[phase], 1 if n % 2 == 0 else 3), core)
        m = 3 + 6 * (phase - 1) + n
        return remote(src, src, ag_send.at[k, m], ag_recv.at[k, m], to)

    def gather_both_ways(k, phase):
        steps = ((0, 0), (0, 1), (0, 1), (0, 0), (3, 0), (1, 1))
        return [gather_ring(k, phase, n, by, half) for n, (by, half) in enumerate(steps)]

    def gather_across(k):
        first, size, order = GATHER[k]
        src = view(codes, {**at, "y": pl.ds(pair, 2), "z": whole()}, slice(None), pl.ds(first, size))
        to = device({**at, "y": lax.rem(at["y"] + 3 - 2 * y_lo, 4)}, core)
        return [remote(src, src, ag_send.at[k, 3], ag_recv.at[k, 3], to)]

    ag_first = [[] if order[0] == "z" else gather_direct(k) for k, (_, _, order) in enumerate(GATHER)]
    ag_mid = [
        gather_across(k) if order[:2] == ("z", "y") else gather_both_ways(k, 1)
        for k, (_, _, order) in enumerate(GATHER)
    ]
    ag_ring = [gather_both_ways(k, 2) for k in range(3)]

    swaps = [remote(cotangent, cot.at[1], swap_send.at[0], swap_recv.at[0], partner)]
    for s in range(SLOTS):
        swaps.append(
            remote(hidden.at[:, hid_cols(s, other)], hid.at[s, 1], swap_send.at[1 + s], swap_recv.at[1 + s], partner)
        )

    peak[0] = jnp.max(
        jnp.abs(own_rows.astype(f32)).reshape(ROWS // 8, 8, WIDTH // 128, 128).max(axis=0), axis=1
    )

    peaks = {}

    def peak_phase(p):
        targets = [partner] if p == 3 else [device(moved(at, AXES[p], j), core) for j in (1, 2, 3)]
        copies = [
            remote(peak.at[p], peak_in.at[p, j], peak_send.at[p, j], peak_recv.at[p, j], to)
            for j, to in enumerate(targets)
        ]
        start(copies)
        peaks[p] = copies

    def peak_join(p):
        best = peak[p]
        for j, copy in enumerate(peaks[p]):
            copy.wait_recv()
            best = jnp.maximum(best, peak_in[p, j])
        peak[p + 1] = best

    def partials():
        @pl.loop(0, SLOTS)
        def _(s):
            pltpu.make_async_copy(hidden.at[:, hid_cols(0, core)], hid.at[s, 0], load_sem.at[2 + s]).wait()
            remote(
                hidden.at[:, hid_cols(0, other)], hid.at[s, 1], swap_send.at[1 + s], swap_recv.at[1 + s], partner
            ).wait_recv()
            term = lax.dot_general(
                hid[s].reshape(2 * TOK, BLOCK), cot[...].reshape(2 * TOK, WIDTH),
                (((0,), (0,)), ((), ())), preferred_element_type=f32,
            )
            partial[s // 2, pl.ds(lax.rem(s, 2) * 2, 2)] = term.astype(bf16).reshape(2, 4, ROWS, WIDTH)

    def ring(k, n, by, half, slot):
        rows, first, size, order = REDUCE[k]
        where = {order[0]: lax.rem(at[order[0]] + by, 4), order[1]: pl.ds(2 * half, 2), order[2]: whole()}
        to = device(moved(at, order[0], 1 if n % 2 == 0 else 3), core)
        return remote(
            view(partial, where, half_rows(rows), pl.ds(first, size)), first_in[k].at[slot],
            rs_send.at[k, n], rs_recv.at[k, n], to,
        )

    rs_ring = [
        [ring(k, 0, 2, 0, 0), ring(k, 1, 2, 1, 1), ring(k, 2, 1, 1, 2), ring(k, 3, 3, 0, 3),
         ring(k, 4, 1, 0, 4), ring(k, 5, 3, 1, 5)]
        for k in range(GROUPS)
    ]

    def part(k, by, half, a, b):
        rows, first, size, order = REDUCE[k]
        where = {order[0]: lax.rem(at[order[0]] + by, 4), order[1]: 2 * half + a, order[2]: b}
        return (where["x"], where["y"], where["z"], half_rows(rows), pl.ds(first, size))

    def add_landed(k, by, half, slots):
        @pl.loop(0, 4)
        def _(b):
            for a in (0, 1):
                index = part(k, by, half, a, b)
                acc = partial[index].astype(f32)
                for slot in slots:
                    acc += first_in[k][spot(k, slot, a, b)].astype(f32)
                partial[index] = acc.astype(bf16)

    def ring_forward(k):
        for n, by, half in ((0, 1, 0), (1, 3, 1)):
            arrive([rs_ring[k][n]])
            add_landed(k, by, half, (n,))
            start([rs_ring[k][4 + n]])

    def reduce_direct(k, phase):
        rows, first, size, order = REDUCE[k]
        landing = second_in if phase == 1 else third_in
        copies = []
        for j in (1, 2, 3):
            where = {order[0]: at[order[0]], order[1]: at[order[1]], order[2]: whole()}
            where[order[phase]] = lax.rem(at[order[phase]] + j, 4)
            n = 6 + (phase - 1) * 3 + j - 1
            copies.append(
                remote(view(partial, where, half_rows(rows), pl.ds(first, size)), landing[k].at[j - 1],
                       rs_send.at[k, n], rs_recv.at[k, n], device(moved(at, order[phase], j), core))
            )
        return copies

    rs_second = [reduce_direct(k, 1) for k in range(GROUPS)]
    rs_third = [reduce_direct(k, 2) for k in range(GROUPS)]

    def ring_end(k):
        arrive(rs_ring[k][2:])
        add_landed(k, 0, 0, (3, 4))
        add_landed(k, 0, 1, (2, 5))
        start(rs_second[k])

    def second_end(k):
        rows, first, size, order = REDUCE[k]
        arrive(rs_second[k])

        @pl.loop(0, 4)
        def _(b):
            where = {order[0]: at[order[0]], order[1]: at[order[1]], order[2]: b}
            index = (where["x"], where["y"], where["z"], half_rows(rows), pl.ds(first, size))
            acc = partial[index].astype(f32)
            for j in range(3):
                acc += second_in[k][j, b].astype(f32)
            partial[index] = acc.astype(bf16)

        start(rs_third[k])

    def piece(half, lo, z):
        row, rows = PARTS[half]
        return pl.ds(pl.multiple_of((lo * 4 + z) * ROWS + row, 16), rows)

    def third_end(k):
        rows, first, size, order = REDUCE[k]
        arrive(rs_third[k])
        acc = partial[at["x"], at["y"], at["z"], half_rows(rows), pl.ds(first, size)].astype(f32)
        for j in range(3):
            acc += third_in[k][j].astype(f32)
        wgrad_out[piece(rows, y_lo, at["z"]), pl.ds(first, size)] = (acc * (32768.0**-0.5)).astype(bf16)

    beside = device({**at, "y": at["y"] + 1 - 2 * y_lo}, core)

    def spread(half, n, rows, to):
        src = wgrad_out.at[rows]
        return remote(src, src, rep_send.at[half, n], rep_recv.at[half, n], to)

    near = [device(moved(at, "z", j), core) for j in (1, 3, 2)]
    rep = []
    for half in (0, 1):
        mine, across = piece(half, y_lo, at["z"]), piece(half, 1 - y_lo, at["z"])
        far = piece(half, y_lo, lax.rem(at["z"] + 2, 4))
        rep.append(
            [spread(half, 0, mine, beside)]
            + [spread(half, 1 + n, mine, to) for n, to in enumerate(near)]
            + [spread(half, 4, across, near[0]), spread(half, 5, across, near[1]), spread(half, 6, far, beside)]
        )

    def spread_more(half):
        arrive(rep[half][:1])
        start(rep[half][4:6])
        arrive(rep[half][3:4])
        start(rep[half][6:7])

    def gather_pass(copies):
        for n in (0, 1):
            arrive([copies[n]])
            start([copies[4 + n]])

    def gather_near(k):
        arrive(ag_mid[k])
        start(ag_ring[k][:2])

    unscale = limit[0] * (1.0 / 448.0)

    last = {order[2]: k for k, (_, _, order) in enumerate(GATHER)}

    def matmuls(n):
        if n == 0:
            for k in range(3):
                arrive(ag_ring[k][:4])
            arrive(ag_ring[last["z"]][4:])
        elif n == 3:
            arrive(ag_ring[last["y"]][4:])
        elif n == 6:
            arrive(ag_ring[last["x"]][4:])
        by, across = ((0, 0), (1, 0), (3, 0), (0, 1), (1, 1), (3, 1), (2, 0), (2, 1))[n]
        x = lax.rem(at["x"] + by, 4)
        y_hi = lax.rem(at["y"] // 2 + across, 2)
        s = x * 2 + y_hi
        w_s = codes[x, pl.ds(y_hi * 2, 2)].reshape(BLOCK, WIDTH)
        h = hid[s].reshape(2 * TOK, BLOCK)
        for c in range(0, WIDTH, 512):
            term = jnp.dot(h, w_s[:, c : c + 512], preferred_element_type=f32)
            keys_acc[:, c : c + 512] = term if n == 0 else keys_acc[:, c : c + 512] + term
        c_all = cot[...].reshape(2 * TOK, WIDTH)
        for c in range(0, BLOCK, 256):
            g = lax.dot_general(c_all, w_s[c : c + 256], (((1,), (1,)), ((), ())), preferred_element_type=f32)
            g = (g * unscale).astype(bf16)
            grad_stage[s, :, c : c + 256] = g[TOK:]
            grad_out[:, pl.ds(pl.multiple_of((s * 2 + core) * BLOCK + c, 256), 256)] = g[:TOK]
        remote(
            grad_stage.at[s], grad_out.at[:, hid_cols(s, core)], grad_send.at[s], grad_recv.at[s], partner
        ).start()
        if n == SLOTS - 1:
            keys_send[...] = keys_acc[TOK:].astype(bf16)
            start([key_copy])

    place_ratio = pltpu.make_async_copy(ratio, ratio_out, load_sem.at[2 + SLOTS])
    key_copy = remote(keys_send, keys_recv, key_send.at[0], key_recv.at[0], partner)

    def step(name, n):
        if name == "gather_first":
            start(ag_first[n])
        elif name == "gather_second":
            arrive(ag_first[n])
            start(ag_mid[n][:4])
        elif name == "gather_second_far":
            if len(ag_mid[n]) > 1:
                gather_pass(ag_mid[n])
        elif name == "gather_near":
            gather_near(n)
        elif name == "gather_rest":
            start(ag_ring[n][2:4])
        elif name == "gather_far":
            gather_pass(ag_ring[n])
        elif name == "swap":
            start(swaps)
        elif name == "partials":
            load_c.wait()
            arrive(swaps[:1])
            partials()
        elif name == "ring_far":
            start(rs_ring[n][:2])
        elif name == "ring_near":
            start(rs_ring[n][2:4])
        elif name == "ring_sum":
            ring_forward(n)
        elif name == "second_axis":
            ring_end(n)
        elif name == "third_axis":
            second_end(n)
        elif name == "spread":
            for k in range(3 * n, 3 * n + 3):
                third_end(k)
            start(rep[n][:4])
        elif name == "spread_more":
            spread_more(n)
        elif name == "spread_end":
            arrive(rep[n])
        elif name == "matmuls":
            matmuls(n)
        elif name == "keys":
            arrive([key_copy])
            keys_out[...] = ((keys_acc[:TOK] + keys_recv[...].astype(f32)) * unscale).astype(bf16)
        elif name == "peak":
            if n > 0:
                peak_join(n - 1)
            if n < 4:
                peak_phase(n)
            else:
                ratio[0] = jnp.max(peak[4] / jnp.full((8, 128), limit[0], f32))
                place_ratio.start()
        else:
            raise ValueError(name)

    for name, n in SCHEDULE:
        step(name, n)

    place_ratio.wait()
    for s in range(SLOTS):
        remote(grad_stage.at[s], grad_out.at[:, hid_cols(s, core)], grad_send.at[s], grad_recv.at[s], partner).wait()
    for copy in sent:
        copy.wait_send()


def place(keys, grad, wgrad, ratio, keys_out, grad_out, wgrad_out, ratio_out, sem):
    copies = [
        pltpu.make_async_copy(src, dst, sem.at[n])
        for n, (src, dst) in enumerate(((grad, grad_out), (wgrad, wgrad_out), (keys, keys_out), (ratio, ratio_out)))
    ]
    for copy in copies:
        copy.start()
    for copy in copies:
        copy.wait()


def landing(k, phase):
    half, _, size, _ = REDUCE[k]
    shape = (spot(k, 6, 2, 4), (3, 4), (3,))[phase]
    return pltpu.VMEM((*shape, PARTS[half][1], size), jnp.bfloat16)


def body(hidden_states, key_weight, previous_peak, key_cotangent):
    bf16, f32 = jnp.bfloat16, jnp.float32
    any_space = pl.BlockSpec(memory_space=pl.ANY)
    hbm = pl.BlockSpec(memory_space=pltpu.HBM)
    vmem = pl.BlockSpec(memory_space=pltpu.VMEM)
    smem = pl.BlockSpec(memory_space=pltpu.SMEM)
    dma = pltpu.SemaphoreType.DMA
    shapes = ((TOK, WIDTH), (TOK, 2 * SLOTS * BLOCK), (BLOCK, WIDTH))
    *results, ratio = pl.pallas_call(
        kernel,
        out_shape=(*[pltpu.VMEM(shape, bf16) for shape in shapes], jax.ShapeDtypeStruct((1,), f32)),
        in_specs=[hbm, hbm, smem, hbm],
        out_specs=(vmem, vmem, vmem, any_space),
        scratch_shapes=[
            pltpu.SMEM((1,), f32),
            pltpu.VMEM((BLOCK, WIDTH), bf16),
            pltpu.VMEM((4, 4, 4, ROWS, WIDTH), bf16),
            pltpu.VMEM((4, 4, 4, ROWS, WIDTH), bf16),
            pltpu.VMEM((SLOTS, 2, TOK, BLOCK), bf16),
            pltpu.VMEM((2, TOK, WIDTH), bf16),
            pltpu.VMEM((2 * TOK, WIDTH), f32),
            pltpu.VMEM((TOK, WIDTH), bf16),
            pltpu.VMEM((TOK, WIDTH), bf16),
            pltpu.VMEM((SLOTS, TOK, BLOCK), bf16),
            pltpu.VMEM((5, 8, 128), f32),
            pltpu.VMEM((4, 3, 8, 128), f32),
            *[landing(k, phase) for phase in range(3) for k in range(GROUPS)],
            dma((3 + SLOTS,)),
            dma((1 + SLOTS,)),
            dma((1 + SLOTS,)),
            dma((3, 15)),
            dma((3, 15)),
            dma((GROUPS, 12)),
            dma((GROUPS, 12)),
            dma((2, 7)),
            dma((2, 7)),
            dma((4, 3)),
            dma((4, 3)),
            dma((1,)),
            dma((1,)),
            dma((SLOTS,)),
            dma((SLOTS,)),
        ],
        compiler_params=pltpu.CompilerParams(
            collective_id=0, has_side_effects=True, vmem_limit_bytes=44 * 2**20
        ),
    )(
        pltpu.with_memory_space_constraint(hidden_states, pltpu.HBM),
        pltpu.with_memory_space_constraint(key_weight, pltpu.HBM),
        previous_peak,
        pltpu.with_memory_space_constraint(key_cotangent, pltpu.HBM),
    )
    return pl.pallas_call(
        place,
        out_shape=(*[jax.ShapeDtypeStruct(shape, bf16) for shape in shapes], jax.ShapeDtypeStruct((1,), f32)),
        in_specs=[any_space] * 4,
        out_specs=(any_space,) * 4,
        scratch_shapes=[dma((4,))],
        compiler_params=pltpu.CompilerParams(vmem_limit_bytes=2**20),
    )(*[pltpu.with_memory_space_constraint(array, pltpu.VMEM) for array in results], ratio)


def solution(mesh):
    in_specs = (P(("replica", "fsdp"), None), P("fsdp", None), P(), P(("replica", "fsdp"), None))
    out_specs = (P(("replica", "fsdp"), None), P(("replica", "fsdp"), None), P("fsdp", None), P())
    return jax.shard_map(body, mesh=mesh, in_specs=in_specs, out_specs=out_specs, check_vma=False)
```

```python
import jax
import jax.numpy as jnp
from jax import lax
from jax.experimental import pallas as pl
from jax.experimental.pallas import tpu as pltpu
from jax.sharding import PartitionSpec as P

MESH = pl.DeviceIdType.MESH
AXES = ("x", "y", "z")
ROWS = 64
WIDTH = 1024
TOK = 256
SLOTS = 8
BLOCK = 512
GATHER = (
    (0, 384, ("z", "y", "x")),
    (384, 384, ("z", "x", "y")),
    (768, 256, ("x", "y", "z")),
)
REDUCE = (
    (0, 0, 384, ("z", "x", "y")),
    (0, 384, 256, ("x", "y", "z")),
    (0, 640, 384, ("y", "z", "x")),
    (1, 0, 384, ("z", "x", "y")),
    (1, 384, 384, ("x", "z", "y")),
    (1, 768, 256, ("y", "z", "x")),
)
SCHEDULE = (
    ("gather_second", 0), ("gather_second", 1), ("gather_first", 2), ("swap", 0), ("peak", 0), ("partials", 0),
    ("peak", 1), ("ring_far", 0), ("ring_far", 3), ("ring_far", 1), ("ring_far", 2), ("ring_far", 4),
    ("ring_far", 5), ("ring_sum", 1), ("ring_near", 0), ("gather_second", 2), ("ring_sum", 5), ("peak", 2),
    ("gather_near", 0), ("gather_second_far", 1), ("ring_sum", 3), ("ring_near", 5), ("ring_near", 1),
    ("ring_sum", 2), ("ring_near", 2), ("ring_near", 3), ("ring_sum", 0), ("gather_second_far", 2),
    ("second_axis", 5), ("ring_near", 4), ("gather_near", 1), ("second_axis", 2), ("second_axis", 1),
    ("ring_sum", 4), ("second_axis", 0), ("second_axis", 3), ("gather_near", 2), ("gather_rest", 1),
    ("third_axis", 5), ("gather_rest", 0), ("gather_rest", 2), ("third_axis", 2), ("third_axis", 0),
    ("gather_far", 2), ("second_axis", 4), ("gather_far", 0), ("gather_far", 1), ("third_axis", 3), ("matmuls", 0),
    ("peak", 3), ("third_axis", 1), ("matmuls", 1), ("matmuls", 2), ("third_axis", 4), ("spread", 0), ("matmuls", 3),
    ("matmuls", 4), ("spread", 1), ("matmuls", 5), ("matmuls", 6), ("spread_more", 0), ("matmuls", 7),
    ("spread_more", 1), ("keys", 0), ("spread_end", 1), ("spread_end", 0), ("peak", 4),
)
GROUPS = len(REDUCE)
PARTS = ((0, 32), (32, 32))


def position():
    replica, fsdp = lax.axis_index("replica"), lax.axis_index("fsdp")
    y_lo, z = replica // 4, lax.rem(replica, 4)
    x, y_hi, core = fsdp // 4, lax.rem(fsdp // 2, 2), lax.rem(fsdp, 2)
    return {"x": x, "y": y_hi * 2 + y_lo, "z": z}, core


def device(at, core):
    y_hi, y_lo = at["y"] // 2, lax.rem(at["y"], 2)
    return (y_lo * 4 + at["z"], at["x"] * 4 + y_hi * 2 + core)


def moved(at, axis, by):
    return {**at, axis: lax.rem(at[axis] + by, 4)}


def whole():
    return pl.ds(0, 4)


def spot(k, slot, a, b):
    order = REDUCE[k][3]
    return (slot, a, b) if AXES.index(order[1]) < AXES.index(order[2]) else (slot, b, a)


def half_rows(half):
    return pl.ds(*PARTS[half])


def kernel(hidden, weight, limit, cotangent, keys_out, grad_out, wgrad_out, ratio_out, *scratch):
    (ratio, w_in, codes, partial, hid, cot, keys_acc, keys_send, keys_recv, grad_stage, peak, peak_in) = scratch[:12]
    landings = scratch[12 : 12 + 3 * GROUPS]
    first_in, second_in, third_in = (landings[n * GROUPS : (n + 1) * GROUPS] for n in range(3))
    (load_sem, swap_send, swap_recv, ag_send, ag_recv, rs_send, rs_recv, rep_send, rep_recv,
     peak_send, peak_recv, key_send, key_recv, grad_send, grad_recv) = scratch[12 + 3 * GROUPS :]

    at, core = position()
    other = 1 - core
    partner = device(at, other)
    f32, bf16 = jnp.float32, jnp.bfloat16
    y_lo = lax.rem(at["y"], 2)

    def remote(src, dst, send, recv, to):
        return pltpu.make_async_remote_copy(
            src_ref=src, dst_ref=dst, send_sem=send, recv_sem=recv, device_id=to, device_id_type=MESH
        )

    sent, landed = [], set()

    def start(copies):
        for copy in copies:
            copy.start()
            sent.append(copy)

    def arrive(copies):
        for copy in copies:
            if id(copy) not in landed:
                landed.add(id(copy))
                copy.wait_recv()

    def hid_cols(slot, which):
        return pl.ds(pl.multiple_of((slot * 2 + which) * BLOCK, BLOCK), BLOCK)

    load_w = pltpu.make_async_copy(weight, w_in, load_sem.at[0])
    load_w.start()
    load_c = pltpu.make_async_copy(cotangent, cot.at[0], load_sem.at[1])
    load_c.start()
    for s in range(SLOTS):
        pltpu.make_async_copy(hidden.at[:, hid_cols(s, core)], hid.at[s, 0], load_sem.at[2 + s]).start()

    barrier = pltpu.get_barrier_semaphore()
    pl.semaphore_signal(barrier, inc=1, device_id=partner, device_id_type=MESH)
    for axis in AXES:
        for j in (1, 2, 3):
            pl.semaphore_signal(barrier, inc=1, device_id=device(moved(at, axis, j), core), device_id_type=MESH)

    load_w.wait()
    lim = jnp.full((1, WIDTH), limit[0], f32)
    scale = 448.0 / lim

    def quantize(w, first, size):
        return jnp.clip(w.astype(f32) * scale[:, first : first + size], -448.0, 448.0).astype(bf16)

    def rows_of(lo, z):
        return pl.ds(pl.multiple_of((lo * 4 + z) * ROWS, ROWS), ROWS)

    own_rows = w_in[rows_of(y_lo, at["z"]), :]
    pair = at["y"] - y_lo
    for first, size, order in GATHER:
        cols = slice(first, first + size)
        if order[:2] == ("z", "y"):
            block = quantize(w_in[:, cols], first, size)
            codes[at["x"], pl.ds(pair, 2), :, :, cols] = block.reshape(2, 4, ROWS, size)
        elif order[0] == "z":
            for z in range(4):
                codes[at["x"], at["y"], z, :, cols] = quantize(w_in[rows_of(y_lo, z), cols], first, size)
        else:
            codes[at["x"], at["y"], at["z"], :, cols] = quantize(own_rows[:, cols], first, size)

    pl.semaphore_wait(barrier, 10)

    def view(ref, where, rows, cols):
        return ref.at[where["x"], where["y"], where["z"], rows, cols]

    def gather_direct(k):
        first, size, order = GATHER[k]
        src = view(codes, at, slice(None), pl.ds(first, size))
        return [
            remote(src, src, ag_send.at[k, j - 1], ag_recv.at[k, j - 1], device(moved(at, order[0], j), core))
            for j in (1, 2, 3)
        ]

    def gather_ring(k, phase, n, by, half):
        first, size, order = GATHER[k]
        where = {order[0]: pl.ds(2 * half, 2), order[1]: whole(), order[2]: at[order[2]]}
        where[order[phase]] = lax.rem(at[order[phase]] + by, 4)
        src = view(codes, where, slice(None), pl.ds(first, size))
        to = device(moved(at, order[phase], 1 if n % 2 == 0 else 3), core)
        m = 3 + 6 * (phase - 1) + n
        return remote(src, src, ag_send.at[k, m], ag_recv.at[k, m], to)

    def gather_both_ways(k, phase):
        steps = ((0, 0), (0, 1), (0, 1), (0, 0), (3, 0), (1, 1))
        return [gather_ring(k, phase, n, by, half) for n, (by, half) in enumerate(steps)]

    def gather_across(k):
        first, size, order = GATHER[k]
        src = view(codes, {**at, "y": pl.ds(pair, 2), "z": whole()}, slice(None), pl.ds(first, size))
        to = device({**at, "y": lax.rem(at["y"] + 3 - 2 * y_lo, 4)}, core)
        return [remote(src, src, ag_send.at[k, 3], ag_recv.at[k, 3], to)]

    ag_first = [[] if order[0] == "z" else gather_direct(k) for k, (_, _, order) in enumerate(GATHER)]
    ag_mid = [
        gather_across(k) if order[:2] == ("z", "y") else gather_both_ways(k, 1)
        for k, (_, _, order) in enumerate(GATHER)
    ]
    ag_ring = [gather_both_ways(k, 2) for k in range(3)]

    swaps = [remote(cotangent, cot.at[1], swap_send.at[0], swap_recv.at[0], partner)]
    for s in range(SLOTS):
        swaps.append(
            remote(hidden.at[:, hid_cols(s, other)], hid.at[s, 1], swap_send.at[1 + s], swap_recv.at[1 + s], partner)
        )

    peak[0] = jnp.max(
        jnp.abs(own_rows.astype(f32)).reshape(ROWS // 8, 8, WIDTH // 128, 128).max(axis=0), axis=1
    )

    peaks = {}

    def peak_phase(p):
        targets = [partner] if p == 3 else [device(moved(at, AXES[p], j), core) for j in (1, 2, 3)]
        copies = [
            remote(peak.at[p], peak_in.at[p, j], peak_send.at[p, j], peak_recv.at[p, j], to)
            for j, to in enumerate(targets)
        ]
        start(copies)
        peaks[p] = copies

    def peak_join(p):
        best = peak[p]
        for j, copy in enumerate(peaks[p]):
            copy.wait_recv()
            best = jnp.maximum(best, peak_in[p, j])
        peak[p + 1] = best

    def partials():
        @pl.loop(0, SLOTS)
        def _(s):
            pltpu.make_async_copy(hidden.at[:, hid_cols(0, core)], hid.at[s, 0], load_sem.at[2 + s]).wait()
            remote(
                hidden.at[:, hid_cols(0, other)], hid.at[s, 1], swap_send.at[1 + s], swap_recv.at[1 + s], partner
            ).wait_recv()
            term = lax.dot_general(
                hid[s].reshape(2 * TOK, BLOCK), cot[...].reshape(2 * TOK, WIDTH),
                (((0,), (0,)), ((), ())), preferred_element_type=f32,
            )
            partial[s // 2, pl.ds(lax.rem(s, 2) * 2, 2)] = term.astype(bf16).reshape(2, 4, ROWS, WIDTH)

    def ring(k, n, by, half, slot):
        rows, first, size, order = REDUCE[k]
        where = {order[0]: lax.rem(at[order[0]] + by, 4), order[1]: pl.ds(2 * half, 2), order[2]: whole()}
        to = device(moved(at, order[0], 1 if n % 2 == 0 else 3), core)
        return remote(
            view(partial, where, half_rows(rows), pl.ds(first, size)), first_in[k].at[slot],
            rs_send.at[k, n], rs_recv.at[k, n], to,
        )

    rs_ring = [
        [ring(k, 0, 2, 0, 0), ring(k, 1, 2, 1, 1), ring(k, 2, 1, 1, 2), ring(k, 3, 3, 0, 3),
         ring(k, 4, 1, 0, 4), ring(k, 5, 3, 1, 5)]
        for k in range(GROUPS)
    ]

    def part(k, by, half, a, b):
        rows, first, size, order = REDUCE[k]
        where = {order[0]: lax.rem(at[order[0]] + by, 4), order[1]: 2 * half + a, order[2]: b}
        return (where["x"], where["y"], where["z"], half_rows(rows), pl.ds(first, size))

    def add_landed(k, by, half, slots):
        @pl.loop(0, 4)
        def _(b):
            for a in (0, 1):
                index = part(k, by, half, a, b)
                acc = partial[index].astype(f32)
                for slot in slots:
                    acc += first_in[k][spot(k, slot, a, b)].astype(f32)
                partial[index] = acc.astype(bf16)

    def ring_forward(k):
        for n, by, half in ((0, 1, 0), (1, 3, 1)):
            arrive([rs_ring[k][n]])
            add_landed(k, by, half, (n,))
            start([rs_ring[k][4 + n]])

    def reduce_direct(k, phase):
        rows, first, size, order = REDUCE[k]
        landing = second_in if phase == 1 else third_in
        copies = []
        for j in (1, 2, 3):
            where = {order[0]: at[order[0]], order[1]: at[order[1]], order[2]: whole()}
            where[order[phase]] = lax.rem(at[order[phase]] + j, 4)
            n = 6 + (phase - 1) * 3 + j - 1
            copies.append(
                remote(view(partial, where, half_rows(rows), pl.ds(first, size)), landing[k].at[j - 1],
                       rs_send.at[k, n], rs_recv.at[k, n], device(moved(at, order[phase], j), core))
            )
        return copies

    rs_second = [reduce_direct(k, 1) for k in range(GROUPS)]
    rs_third = [reduce_direct(k, 2) for k in range(GROUPS)]

    def ring_end(k):
        arrive(rs_ring[k][2:])
        add_landed(k, 0, 0, (3, 4))
        add_landed(k, 0, 1, (2, 5))
        start(rs_second[k])

    def second_end(k):
        rows, first, size, order = REDUCE[k]
        arrive(rs_second[k])

        @pl.loop(0, 4)
        def _(b):
            where = {order[0]: at[order[0]], order[1]: at[order[1]], order[2]: b}
            index = (where["x"], where["y"], where["z"], half_rows(rows), pl.ds(first, size))
            acc = partial[index].astype(f32)
            for j in range(3):
                acc += second_in[k][j, b].astype(f32)
            partial[index] = acc.astype(bf16)

        start(rs_third[k])

    def piece(half, lo, z):
        row, rows = PARTS[half]
        return pl.ds(pl.multiple_of((lo * 4 + z) * ROWS + row, 16), rows)

    def third_end(k):
        rows, first, size, order = REDUCE[k]
        arrive(rs_third[k])
        acc = partial[at["x"], at["y"], at["z"], half_rows(rows), pl.ds(first, size)].astype(f32)
        for j in range(3):
            acc += third_in[k][j].astype(f32)
        wgrad_out[piece(rows, y_lo, at["z"]), pl.ds(first, size)] = (acc * (32768.0**-0.5)).astype(bf16)

    beside = device({**at, "y": at["y"] + 1 - 2 * y_lo}, core)

    def spread(half, n, rows, to):
        src = wgrad_out.at[rows]
        return remote(src, src, rep_send.at[half, n], rep_recv.at[half, n], to)

    near = [device(moved(at, "z", j), core) for j in (1, 3, 2)]
    rep = []
    for half in (0, 1):
        mine, across = piece(half, y_lo, at["z"]), piece(half, 1 - y_lo, at["z"])
        far = piece(half, y_lo, lax.rem(at["z"] + 2, 4))
        rep.append(
            [spread(half, 0, mine, beside)]
            + [spread(half, 1 + n, mine, to) for n, to in enumerate(near)]
            + [spread(half, 4, across, near[0]), spread(half, 5, across, near[1]), spread(half, 6, far, beside)]
        )

    def spread_more(half):
        arrive(rep[half][:1])
        start(rep[half][4:6])
        arrive(rep[half][3:4])
        start(rep[half][6:7])

    def gather_pass(copies):
        for n in (0, 1):
            arrive([copies[n]])
            start([copies[4 + n]])

    def gather_near(k):
        arrive(ag_mid[k])
        start(ag_ring[k][:2])

    unscale = limit[0] * (1.0 / 448.0)

    last = {order[2]: k for k, (_, _, order) in enumerate(GATHER)}

    def matmuls(n):
        if n == 0:
            for k in range(3):
                arrive(ag_ring[k][:4])
            arrive(ag_ring[last["z"]][4:])
        elif n == 3:
            arrive(ag_ring[last["y"]][4:])
        elif n == 6:
            arrive(ag_ring[last["x"]][4:])
        by, across = ((0, 0), (1, 0), (3, 0), (0, 1), (1, 1), (3, 1), (2, 0), (2, 1))[n]
        x = lax.rem(at["x"] + by, 4)
        y_hi = lax.rem(at["y"] // 2 + across, 2)
        s = x * 2 + y_hi
        w_s = codes[x, pl.ds(y_hi * 2, 2)].reshape(BLOCK, WIDTH)
        h = hid[s].reshape(2 * TOK, BLOCK)
        for c in range(0, WIDTH, 512):
            term = jnp.dot(h, w_s[:, c : c + 512], preferred_element_type=f32)
            keys_acc[:, c : c + 512] = term if n == 0 else keys_acc[:, c : c + 512] + term
        c_all = cot[...].reshape(2 * TOK, WIDTH)
        for c in range(0, BLOCK, 256):
            g = lax.dot_general(c_all, w_s[c : c + 256], (((1,), (1,)), ((), ())), preferred_element_type=f32)
            g = (g * unscale).astype(bf16)
            grad_stage[s, :, c : c + 256] = g[TOK:]
            grad_out[:, pl.ds(pl.multiple_of((s * 2 + core) * BLOCK + c, 256), 256)] = g[:TOK]
        remote(
            grad_stage.at[s], grad_out.at[:, hid_cols(s, core)], grad_send.at[s], grad_recv.at[s], partner
        ).start()
        if n == SLOTS - 1:
            keys_send[...] = keys_acc[TOK:].astype(bf16)
            start([key_copy])

    place_ratio = pltpu.make_async_copy(ratio, ratio_out, load_sem.at[2 + SLOTS])
    key_copy = remote(keys_send, keys_recv, key_send.at[0], key_recv.at[0], partner)

    def step(name, n):
        if name == "gather_first":
            start(ag_first[n])
        elif name == "gather_second":
            arrive(ag_first[n])
            start(ag_mid[n][:4])
        elif name == "gather_second_far":
            if len(ag_mid[n]) > 1:
                gather_pass(ag_mid[n])
        elif name == "gather_near":
            gather_near(n)
        elif name == "gather_rest":
            start(ag_ring[n][2:4])
        elif name == "gather_far":
            gather_pass(ag_ring[n])
        elif name == "swap":
            start(swaps)
        elif name == "partials":
            load_c.wait()
            arrive(swaps[:1])
            partials()
        elif name == "ring_far":
            start(rs_ring[n][:2])
        elif name == "ring_near":
            start(rs_ring[n][2:4])
        elif name == "ring_sum":
            ring_forward(n)
        elif name == "second_axis":
            ring_end(n)
        elif name == "third_axis":
            second_end(n)
        elif name == "spread":
            for k in range(3 * n, 3 * n + 3):
                third_end(k)
            start(rep[n][:4])
        elif name == "spread_more":
            spread_more(n)
        elif name == "spread_end":
            arrive(rep[n])
        elif name == "matmuls":
            matmuls(n)
        elif name == "keys":
            arrive([key_copy])
            leave()
            keys_out[...] = ((keys_acc[:TOK] + keys_recv[...].astype(f32)) * unscale).astype(bf16)
        elif name == "peak":
            if n > 0:
                peak_join(n - 1)
            if n < 4:
                peak_phase(n)
            else:
                ratio[0] = jnp.max(peak[4] / jnp.full((8, 128), limit[0], f32))
                place_ratio.start()
        else:
            raise ValueError(name)

    def leave():
        for s in range(SLOTS):
            remote(
                grad_stage.at[s], grad_out.at[:, hid_cols(s, core)], grad_send.at[s], grad_recv.at[s], partner
            ).wait()
        last = {id(copy) for half in (0, 1) for copy in rep[half]}
        for copy in sent:
            if id(copy) not in last:
                copy.wait_send()
        sent[:] = [copy for copy in sent if id(copy) in last]

    for name, n in SCHEDULE:
        step(name, n)

    place_ratio.wait()
    for copy in sent:
        copy.wait_send()


def place(keys, grad, wgrad, ratio, keys_out, grad_out, wgrad_out, ratio_out, sem):
    copies = [
        pltpu.make_async_copy(src, dst, sem.at[n])
        for n, (src, dst) in enumerate(((grad, grad_out), (wgrad, wgrad_out), (keys, keys_out), (ratio, ratio_out)))
    ]
    for copy in copies:
        copy.start()
    for copy in copies:
        copy.wait()


def landing(k, phase):
    half, _, size, _ = REDUCE[k]
    shape = (spot(k, 6, 2, 4), (3, 4), (3,))[phase]
    return pltpu.VMEM((*shape, PARTS[half][1], size), jnp.bfloat16)


def body(hidden_states, key_weight, previous_peak, key_cotangent):
    bf16, f32 = jnp.bfloat16, jnp.float32
    any_space = pl.BlockSpec(memory_space=pl.ANY)
    hbm = pl.BlockSpec(memory_space=pltpu.HBM)
    vmem = pl.BlockSpec(memory_space=pltpu.VMEM)
    smem = pl.BlockSpec(memory_space=pltpu.SMEM)
    dma = pltpu.SemaphoreType.DMA
    shapes = ((TOK, WIDTH), (TOK, 2 * SLOTS * BLOCK), (BLOCK, WIDTH))
    *results, ratio = pl.pallas_call(
        kernel,
        out_shape=(*[pltpu.VMEM(shape, bf16) for shape in shapes], jax.ShapeDtypeStruct((1,), f32)),
        in_specs=[hbm, hbm, smem, hbm],
        out_specs=(vmem, vmem, vmem, any_space),
        scratch_shapes=[
            pltpu.SMEM((1,), f32),
            pltpu.VMEM((BLOCK, WIDTH), bf16),
            pltpu.VMEM((4, 4, 4, ROWS, WIDTH), bf16),
            pltpu.VMEM((4, 4, 4, ROWS, WIDTH), bf16),
            pltpu.VMEM((SLOTS, 2, TOK, BLOCK), bf16),
            pltpu.VMEM((2, TOK, WIDTH), bf16),
            pltpu.VMEM((2 * TOK, WIDTH), f32),
            pltpu.VMEM((TOK, WIDTH), bf16),
            pltpu.VMEM((TOK, WIDTH), bf16),
            pltpu.VMEM((SLOTS, TOK, BLOCK), bf16),
            pltpu.VMEM((5, 8, 128), f32),
            pltpu.VMEM((4, 3, 8, 128), f32),
            *[landing(k, phase) for phase in range(3) for k in range(GROUPS)],
            dma((3 + SLOTS,)),
            dma((1 + SLOTS,)),
            dma((1 + SLOTS,)),
            dma((3, 15)),
            dma((3, 15)),
            dma((GROUPS, 12)),
            dma((GROUPS, 12)),
            dma((2, 7)),
            dma((2, 7)),
            dma((4, 3)),
            dma((4, 3)),
            dma((1,)),
            dma((1,)),
            dma((SLOTS,)),
            dma((SLOTS,)),
        ],
        compiler_params=pltpu.CompilerParams(
            collective_id=0, has_side_effects=True, vmem_limit_bytes=44 * 2**20
        ),
    )(
        pltpu.with_memory_space_constraint(hidden_states, pltpu.HBM),
        pltpu.with_memory_space_constraint(key_weight, pltpu.HBM),
        previous_peak,
        pltpu.with_memory_space_constraint(key_cotangent, pltpu.HBM),
    )
    return pl.pallas_call(
        place,
        out_shape=(*[jax.ShapeDtypeStruct(shape, bf16) for shape in shapes], jax.ShapeDtypeStruct((1,), f32)),
        in_specs=[any_space] * 4,
        out_specs=(any_space,) * 4,
        scratch_shapes=[dma((4,))],
        compiler_params=pltpu.CompilerParams(vmem_limit_bytes=2**20),
    )(*[pltpu.with_memory_space_constraint(array, pltpu.VMEM) for array in results], ratio)


def solution(mesh):
    in_specs = (P(("replica", "fsdp"), None), P("fsdp", None), P(), P(("replica", "fsdp"), None))
    out_specs = (P(("replica", "fsdp"), None), P(("replica", "fsdp"), None), P("fsdp", None), P())
    return jax.shard_map(body, mesh=mesh, in_specs=in_specs, out_specs=out_specs, check_vma=False)
```
